256 devices in a mesh: lat: 16 (over z, core), lon: 16 (over y, x).
Axes of the slice: x: 4, y: 4, z: 8, core: 2. Of those that a mesh axis runs over, the one named last changes fastest.
Arguments:
- increments: float32 [2, 8, 512, 6144], P(None, None, 'lat', 'lon'), may hold values from -4 to 4
- ens_winds: bfloat16 [2, 8, 128, 1536], P(None, None, 'lat', 'lon'), may hold values from -6 to 6
- lat_offsets: int32 [16], P('lat'), may hold values from 4 to 116, as said below
- lon_offsets: int32 [16], P('lon'), may hold values from -4 to 1444, as said below
Outputs:
- potentials: float32 [2, 8, 512, 6144], P(None, None, 'lat', 'lon')
The draws below stay inside these ranges and needn't reach their ends.
Inputs may be any that keep to these rules, and one draw needn't show every extreme that they name: `lat_offsets`: the offset of tile row i is i * 8 plus a jitter of at most 4 in size; the first tile row's jitter is exactly +4, the last one's exactly -4. `lon_offsets`: the offset of tile column j is j * 96 plus a jitter of at most 4 in size; the first tile column's jitter is exactly -4, the last one's exactly +4; columns are read modulo 1536.
All inputs are finite; a program needn't handle non-finite values.
Results may differ from the reference program's by a relative error of at most 0.0009.
Values may be sent and summed in bfloat16 or wider, within the bound.
No kernel may reach another device: no remote copies, remote signals or barrier semaphores. Data moves between devices by JAX's collectives and lax.ppermute only.
A program may use at most 128 MiB of HBM per device.

```python
import jax
import jax.numpy as jnp

LEV = 8
FIELDS = 2
CLAT = 32
CLON = 384
GRIDS = 5
SWEEPS = 2
COARSE_SWEEPS = 4
CYCLES = 2
EROW = 8
ECOL = 96
JITTER = 4
NLAT = 512
NLON = 6144
ELAT = 128
ELON = 1536
LAT_TILES = 16
LON_TILES = 16


def draw_increments(key, part):
    key = jax.random.fold_in(key, 5)
    full_shape = (FIELDS, LEV, NLAT, NLON)
    return jax.random.truncated_normal(key, -4.0, 4.0, full_shape, jnp.float32)


def draw_lat_offsets(key, part):
    key = jax.random.fold_in(key, 7)
    tile_ids = jnp.arange(LAT_TILES, dtype=jnp.int32)
    jitter_draw = jax.random.randint(key, (LAT_TILES,), -JITTER, JITTER + 1, dtype=jnp.int32)
    jitter_draw = jnp.where(tile_ids == 0, JITTER, jnp.where(tile_ids == LAT_TILES - 1, -JITTER, jitter_draw))
    return (tile_ids * EROW + jitter_draw).astype(jnp.int32)


def draw_lon_offsets(key, part):
    key = jax.random.fold_in(key, 9)
    tile_ids = jnp.arange(LON_TILES, dtype=jnp.int32)
    jitter_draw = jax.random.randint(key, (LON_TILES,), -JITTER, JITTER + 1, dtype=jnp.int32)
    jitter_draw = jnp.where(tile_ids == 0, -JITTER, jnp.where(tile_ids == LON_TILES - 1, JITTER, jitter_draw))
    return (tile_ids * ECOL + jitter_draw).astype(jnp.int32)


def shard_levels(key, dims, pieces, least, high):
    level = 1.0
    for position, shards_of in pieces:
        steps = jax.random.uniform(jax.random.fold_in(jax.random.fold_in(key, 6), position), (shards_of,), jnp.float32, least / len(pieces), high / len(pieces))
        level = level * jnp.repeat(jnp.exp(steps), dims[position] // shards_of).reshape((-1,) + (1,) * (len(dims) - 1 - position))
    return level


def centred(rng, shape, spread, limit, split=(), kind=jnp.bfloat16):
    factor_of = shard_levels(rng, shape, split, -0.22, 0.18) if split else 1.0
    drawn = jax.random.normal(rng, shape, jnp.float32) * spread * factor_of
    return jnp.minimum(jnp.maximum(drawn, -limit), limit).astype(kind)


def setup_inputs(seed: int = 0) -> dict:
    seeds = jax.random.split(jax.random.key(seed), 5)
    increments = draw_increments(jax.random.fold_in(seeds[4], 71), 0)
    ens_winds = centred(seeds[1], (2, LEV, ELAT, ELON), 1.0, 6.0, ((2, 16), (3, 16)))
    lat_offsets = draw_lat_offsets(jax.random.fold_in(seeds[4], 71), 0)
    lon_offsets = draw_lon_offsets(jax.random.fold_in(seeds[4], 71), 0)
    return dict(increments=increments, ens_winds=ens_winds, lat_offsets=lat_offsets, lon_offsets=lon_offsets)


OMEGA = 0.8


def level_terms(grid_level):
    spacing = 4.0 ** grid_level
    damping = 0.25 / (CLAT * CLAT)
    centre_weight = 4.0 + damping * spacing
    return spacing, centre_weight, OMEGA * spacing / centre_weight


def neighbours(values):
    padded = jnp.pad(values, ((0, 0), (0, 0), (1, 1), (0, 0)))
    return padded[:, :, 2:] + padded[:, :, :-2] + jnp.roll(values, 1, axis=3) + jnp.roll(values, -1, axis=3)


def operate(values, grid_level):
    spacing, centre_weight, factor = level_terms(grid_level)
    return (centre_weight * values - neighbours(values)) / spacing


def smooth(estimate, source, grid_level):
    spacing, centre_weight, factor = level_terms(grid_level)
    return estimate + factor * (source - operate(estimate, grid_level))


def restrict(values):
    fields, levels, row_count, col_count = values.shape
    blocks = values.reshape(fields, levels, row_count // 2, 2, col_count // 2, 2)
    return jnp.sum(blocks, axis=(3, 5)) * 0.25


def prolong(values):
    return jnp.repeat(jnp.repeat(values, 2, axis=2), 2, axis=3)


def vcycle(grid_level, source, estimate):
    if grid_level == GRIDS - 1:
        for turn_index in range(COARSE_SWEEPS):
            estimate = smooth(estimate, source, grid_level)
        return estimate
    for turn_index in range(SWEEPS):
        estimate = smooth(estimate, source, grid_level)
    residual = source - operate(estimate, grid_level)
    coarse = restrict(residual)
    estimate = estimate + prolong(vcycle(grid_level + 1, coarse, jnp.zeros_like(coarse)))
    for turn_index in range(SWEEPS):
        estimate = smooth(estimate, source, grid_level)
    return estimate


def prolong_winds(ens_winds, lat_offsets, lon_offsets):
    row_ids = jnp.arange(NLAT, dtype=jnp.int32)
    tile_rows = row_ids // CLAT
    inside_rows = row_ids % CLAT
    first_row = (lat_offsets[tile_rows] + inside_rows // 4).astype(jnp.int32)
    row_frac = (inside_rows % 4).astype(jnp.float32) * 0.25
    widened = ens_winds.astype(jnp.float32)
    lower_rows = jnp.take(widened, first_row, axis=2)
    upper_rows = jnp.take(widened, first_row + 1, axis=2)
    lat_winds = ((1.0 - row_frac)[:, None] * lower_rows + row_frac[:, None] * upper_rows).astype(jnp.bfloat16)
    col_ids = jnp.arange(NLON, dtype=jnp.int32)
    tile_cols = col_ids // CLON
    inside_cols = col_ids % CLON
    first_col = ((lon_offsets[tile_cols] + inside_cols // 4) % ELON).astype(jnp.int32)
    next_col = ((first_col + 1) % ELON).astype(jnp.int32)
    col_frac = (inside_cols % 4).astype(jnp.float32) * 0.25
    lat_wide = lat_winds.astype(jnp.float32)
    return (1.0 - col_frac) * jnp.take(lat_wide, first_col, axis=3) + col_frac * jnp.take(lat_wide, next_col, axis=3)


def across(values):
    return jnp.roll(values, -1, axis=2) - jnp.roll(values, 1, axis=2)


def along(values):
    padded = jnp.pad(values, ((0, 0), (1, 1), (0, 0)))
    return padded[:, 2:] - padded[:, :-2]


def reference(increments, ens_winds, lat_offsets, lon_offsets):
    fine = prolong_winds(ens_winds, lat_offsets, lon_offsets)
    east_wind = fine[0]
    north_wind = fine[1]
    forcing = increments + 2.0 * jnp.stack([across(north_wind) - along(east_wind), across(east_wind) + along(north_wind)])
    estimate = jnp.zeros_like(forcing)
    for cycle_index in range(CYCLES):
        estimate = vcycle(0, forcing, estimate)
    return estimate
```

```python
import functools

import jax
import jax.numpy as jnp
import ml_dtypes
import numpy as np
from jax import lax
from jax.experimental import pallas as pl
from jax.experimental.pallas import tpu as pltpu
from jax.sharding import PartitionSpec as P

CLAT = 32
GRIDS = 5
OMEGA = 0.8
CYCLES = 2
ROWS = 64
PHASES = 8
LEAD = 40
INC_SCALE = 2.0**13
WIND_SCALE = 2.0**12
OUT_EXP = 14.0
OWN_ROWS = 112
HALO_ROWS = 80

f32 = jnp.float32
bf16 = jnp.bfloat16


def column_of(n):
    return 8 * (n % 128 - LEAD) + n // 128


def spread_table():
    columns = column_of(np.arange(1024))
    return (np.arange(896)[:, None] - 256 == columns[None, :]).astype(ml_dtypes.bfloat16)


def collect_table():
    columns = column_of(np.arange(1024))
    return (columns[:, None] == np.arange(384)[None, :]).astype(ml_dtypes.bfloat16)


def centre(level):
    return 4.0 + 4.0**level * 0.25 / (CLAT * CLAT)


def west(v, hop):
    first = pltpu.roll(v[-1], hop, 1)[None]
    return jnp.concatenate([first, v[:-1]], 0) if v.shape[0] > 1 else first


def east(v, hop):
    last = pltpu.roll(v[0], 128 - hop, 1)[None]
    return jnp.concatenate([v[1:], last], 0) if v.shape[0] > 1 else last


def above_first(v):
    lanes = lax.broadcasted_iota(jnp.int32, (8, 128), 0)
    return jnp.stack([jnp.where(lanes > 0, pltpu.roll(v[p], 1, 0), 0.0) for p in range(v.shape[0])])


def below_last(v):
    lanes = lax.broadcasted_iota(jnp.int32, (8, 128), 0)
    return jnp.stack([jnp.where(lanes < 7, pltpu.roll(v[p], 7, 0), 0.0) for p in range(v.shape[0])])


def doubled(v, phases):
    if v.shape[0] == phases:
        return v
    return jnp.concatenate([v[p // 2][None] for p in range(phases)], 0)


def loop(count, body, carry, unroll):
    if unroll >= count:
        for step in range(count):
            carry = body(step, carry)
        return carry
    return lax.fori_loop(0, count, body, carry, unroll=unroll)


def shape_of(level):
    return ROWS >> level, max(PHASES >> level, 1), (2 if level == GRIDS - 1 else 1)


UNROLL = (2, 4, 8, 4, 2)


def sweep(level, x, b, start=None, coarse=None):
    rows, phases, hop = shape_of(level)
    gain = OMEGA / centre(level)
    if start is not None:
        old = lambda r, s: b[r] * gain
    elif coarse is not None:
        old = lambda r, s: x[r] + doubled(coarse[s], phases)
    else:
        old = lambda r, s: x[r]
    first = old(0, 0)
    top = above_first(old(rows - 1, rows // 2 - 1))
    if start is None:
        x[rows] = below_last(first)

    def body(s, carry):
        prev, c0 = carry
        c1 = old(2 * s + 1, s)
        n = old(2 * s + 2, s + 1)
        x[2 * s] = 0.2 * c0 + gain * ((b[2 * s] + prev) + c1 + (west(c0, hop) + east(c0, hop)))
        x[2 * s + 1] = 0.2 * c1 + gain * ((b[2 * s + 1] + c0) + n + (west(c1, hop) + east(c1, hop)))
        return c1, n

    loop(rows // 2, body, (top, first), UNROLL[level])


def residual(level, x, b, out):
    rows, phases, hop = shape_of(level)
    weight = centre(level)
    first = x[0]
    top = above_first(x[rows - 1])
    x[rows] = below_last(first)

    def body(s, carry):
        prev, c0 = carry
        c1 = x[2 * s + 1]
        n = x[2 * s + 2]
        r0 = (b[2 * s] + prev) + (c1 + (west(c0, hop) + east(c0, hop))) - weight * c0
        r1 = (b[2 * s + 1] + c0) + (n + (west(c1, hop) + east(c1, hop))) - weight * c1
        t = r0 + r1
        if phases > 1:
            out[s] = jnp.concatenate([(t[2 * p] + t[2 * p + 1])[None] for p in range(phases // 2)], 0)
        else:
            lane = lax.broadcasted_iota(jnp.int32, (8, 128), 1)
            out[s] = t + jnp.where(lane % 2 == 0, pltpu.roll(t[0], 127, 1), pltpu.roll(t[0], 1, 1))[None]
        return c1, n

    loop(rows // 2, body, (top, first), UNROLL[level])
    out[rows // 2] = below_last(out[0])


def vcycle(level, x, b, fresh):
    rows = shape_of(level)[0]
    if level == GRIDS - 1:
        sweep(level, x[level], b[level], start=True)
        sweep(level, x[level], b[level])
    else:
        if fresh:
            sweep(level, x[level], b[level], start=True)
        else:
            sweep(level, x[level], b[level])
            sweep(level, x[level], b[level])
        residual(level, x[level], b[level], b[level + 1])
        vcycle(level + 1, x, b, True)
        sweep(level, x[level], b[level], coarse=x[level + 1])
    sweep(level, x[level], b[level])
    if level > 0:
        x[level][rows] = jnp.zeros(x[level].shape[1:], f32)


def hat(position, index):
    return jnp.maximum(1.0 - jnp.abs(position - index), 0.0)


def kernel(own, left, right, spread, collect, out, x0, x1, x2, x3, x4, b0, b1, b2, b3, b4, inc, gx, gy, split):
    x = (x0, x1, x2, x3, x4)
    b = (b0, b1, b2, b3, b4)
    pieces = ((left, 0, HALO_ROWS), (left, 48, HALO_ROWS), (own, 0, OWN_ROWS), (own, 32, OWN_ROWS), (own, 80, OWN_ROWS), (right, 0, HALO_ROWS), (right, 32, HALO_ROWS))
    for j, (ref, at, height) in enumerate(pieces):
        block = jnp.concatenate([ref[i * height + at : i * height + at + 32, :] for i in range(16)], 0) * (1.0 / INC_SCALE)
        high = block.astype(bf16)
        split[0:512, 128 * j : 128 * j + 128] = high
        split[512:1024, 128 * j : 128 * j + 128] = (block - high.astype(f32)).astype(bf16)
    for p in range(PHASES):
        table = spread[:, 128 * p : 128 * p + 128]
        inc[512 * p : 512 * p + 512, :] = jnp.dot(split[0:512, 0:896], table, preferred_element_type=f32) + jnp.dot(
            split[512:1024, 0:896], table, preferred_element_type=f32
        )
    lane = lax.broadcasted_iota(jnp.int32, (8, 128), 1).astype(f32)
    parts = []
    for half in range(2):
        first = own[pl.ds(OWN_ROWS * half + 64, 8, stride=2 * OWN_ROWS), :][:, 96:97]
        for a in range(32):
            parts.append(hat(first + a * 0.25, lane))
    row_table = jnp.concatenate(parts, 0).astype(bf16)

    def winds(offset):
        cols = []
        for ref, at, height in ((left, 32, HALO_ROWS), (own, 64, OWN_ROWS), (right, 64, HALO_ROWS)):
            rows = [ref[i * height + at + offset : i * height + at + offset + 8, :] for i in range(16)]
            cols.append(jnp.concatenate(rows, 0) * (1.0 / WIND_SCALE))
        table = jnp.concatenate(cols, 1).astype(bf16)
        return jnp.dot(row_table, table, preferred_element_type=f32).astype(bf16)

    wx = winds(0)
    wy = winds(8)
    n = lax.broadcasted_iota(jnp.int32, (1, 1024), 1)
    column = 8 * ((n & 127) - LEAD) + (n >> 7)
    shift_left = left[32:33, 97:98]
    shift_own = own[64:65, 97:98]
    shift_right = right[64:65, 97:98]

    def place(c):
        value = c.astype(f32) * 0.25
        return value + 96.0 + jnp.where(c < 0, shift_left, jnp.where(c < 384, shift_own, shift_right))

    m = lax.broadcasted_iota(jnp.int32, (384, 1), 0)
    index = jnp.where((m & 127) < 96, (m >> 7) * 96 + (m & 127), -1000).astype(f32)
    here = place(column)
    gx[...] = jnp.dot(
        wx, (2.0 * (hat(place(column + 1), index) - hat(place(column - 1), index))).astype(bf16), preferred_element_type=f32
    )
    gy[...] = jnp.dot(wy, (2.0 * hat(here, index)).astype(bf16), preferred_element_type=f32)

    def cut(ref, r):
        rows = pl.ds(pl.multiple_of(8 * r, 8), 8)
        return jnp.stack([ref[rows, 128 * p : 128 * p + 128] for p in range(PHASES)])

    def force(r, above, below):
        mine = jnp.stack([inc[pl.ds(512 * p + r, 8, stride=64), :] for p in range(PHASES)])
        b0[r] = mine + cut(gx, r) + (below - above)

    first = cut(gy, 0)
    final = cut(gy, ROWS - 1)

    def force_row(r, carry):
        above, here = carry
        below = cut(gy, r + 1)
        force(r, above, below)
        return here, below

    above, _ = lax.fori_loop(0, ROWS - 1, force_row, (above_first(final), first))
    force(ROWS - 1, above, below_last(first))
    b0[ROWS] = below_last(b0[0])

    for cycle in range(CYCLES):
        vcycle(0, x, b, cycle == 0)

    def peak(r, carry):
        return jnp.maximum(carry, jnp.max(jnp.abs(x0[r]), axis=0))

    top = lax.fori_loop(0, ROWS, peak, jnp.zeros((8, 128), f32))
    lane = lax.broadcasted_iota(jnp.int32, (8, 128), 1)
    top = jnp.max(jnp.where((lane >= LEAD) & (lane < LEAD + 48), top, 0.0), axis=(0, 1), keepdims=True)
    power = jnp.ceil(jnp.log2(jnp.maximum(top, 1e-30)))
    scale = jnp.exp2(OUT_EXP - power)

    def pack(s, carry):
        pair = jnp.concatenate([x0[2 * s], x0[2 * s + 1]], 1) * scale
        high = pair.astype(bf16)
        low = (pair - high.astype(f32)).astype(bf16)
        at = pl.multiple_of(16 * s, 16)
        for p in range(PHASES):
            split[pl.ds(at, 16), 128 * p : 128 * p + 128] = high[p]
            split[pl.ds(at + 512, 16), 128 * p : 128 * p + 128] = low[p]
        return carry

    lax.fori_loop(0, ROWS // 2, pack, 0)
    for j in range(3):
        table = collect[:, 128 * j : 128 * j + 128]
        block = jnp.dot(split[0:512, :], table, preferred_element_type=f32) + jnp.dot(
            split[512:1024, :], table, preferred_element_type=f32
        )
        for r in range(ROWS):
            out[pl.ds(OWN_ROWS * (r // 32) + 32 * j + r % 32, 8, stride=2 * OWN_ROWS), :] = block[8 * r : 8 * r + 8, :]
    for i in range(16):
        out[OWN_ROWS * i + 96 : OWN_ROWS * i + 112, :] = jnp.broadcast_to(power, (16, 128))


def core(own, left, right, interpret=False):
    grids = []
    for level in range(GRIDS):
        rows, phases, _ = shape_of(level)
        grids.append(pltpu.VMEM((rows + 1, phases, 8, 128), f32))
    return pl.pallas_call(
        kernel,
        out_shape=jax.ShapeDtypeStruct((16 * OWN_ROWS, 128), f32),
        scratch_shapes=grids
        + grids
        + [
            pltpu.VMEM((512 * PHASES, 128), f32),
            pltpu.VMEM((512, 1024), f32),
            pltpu.VMEM((512, 1024), f32),
            pltpu.VMEM((1024, 1024), bf16),
        ],
        compiler_params=pltpu.CompilerParams(vmem_limit_bytes=48 * 1024 * 1024),
        interpret=interpret,
    )(own, left, right, jnp.asarray(spread_table()), jnp.asarray(collect_table()))


def parcel(increments, ens_winds, lat_first, lon_shift):
    inc = increments.reshape(16, 32, 384) * INC_SCALE
    u, v = ens_winds[0], ens_winds[1]
    across = jnp.concatenate([v, u], 0)
    along = jnp.concatenate([-u, v], 0)
    winds = jnp.concatenate([across, along], 1).astype(f32) * WIND_SCALE
    lane = lax.broadcasted_iota(jnp.int32, (16, 16, 32), 2)
    meta = jnp.where(lane == 0, lat_first, jnp.where(lane == 1, lon_shift, 0)).astype(f32)
    winds = jnp.concatenate([winds, meta], 2)
    return jnp.concatenate([inc[:, :, 0:128], inc[:, :, 128:256], winds, inc[:, :, 256:384]], 1).astype(jnp.float16)


def unpack(got):
    power = got[:, 96:97, 0:1].astype(f32)
    values = got[:, :96].astype(f32) * jnp.exp2(power - OUT_EXP)
    return values.reshape(16, 3, 32, 128).transpose(0, 2, 1, 3).reshape(2, 8, 32, 384)


def local(increments, ens_winds, lat_offsets, lon_offsets):
    count = lax.axis_size("lon")
    me = lax.axis_index("lon")
    mine = parcel(increments, ens_winds, lat_offsets[0], lon_offsets[0] - me * ens_winds.shape[3])
    held = lax.all_to_all(mine, "lat", 0, 0, tiled=True)
    even = me % 2 == 0
    to_right, to_left = held[:, 32:112], held[:, 0:80]
    pairs0 = [(i, i ^ 1) for i in range(count)]
    pairs1 = [(i, (((i - 1) ^ 1) + 1) % count) for i in range(count)]
    got0 = lax.ppermute(jnp.where(even, to_right, to_left), "lon", pairs0)
    got1 = lax.ppermute(jnp.where(even, to_left, to_right), "lon", pairs1)
    left = jnp.where(even, got1, got0).astype(f32).reshape(16 * HALO_ROWS, 128)
    right = jnp.where(even, got0, got1).astype(f32).reshape(16 * HALO_ROWS, 128)
    own = held.astype(f32).reshape(16 * OWN_ROWS, 128)
    done = core(own, left, right).reshape(16, OWN_ROWS, 128).astype(jnp.float16)
    return unpack(lax.all_to_all(done, "lat", 0, 0, tiled=True))


def solution(mesh):
    in_specs = (P(None, None, "lat", "lon"), P(None, None, "lat", "lon"), P("lat"), P("lon"))
    out_specs = P(None, None, "lat", "lon")
    return jax.shard_map(local, mesh=mesh, in_specs=in_specs, out_specs=out_specs, check_vma=False)
```

```python
import functools

import jax
import jax.numpy as jnp
import ml_dtypes
import numpy as np
from jax import lax
from jax.experimental import pallas as pl
from jax.experimental.pallas import tpu as pltpu
from jax.sharding import PartitionSpec as P

CLAT = 32
GRIDS = 5
OMEGA = 0.8
CYCLES = 2
ROWS = 64
PHASES = 8
LEAD = 40
IN_EXP = 14.0
GAIN_EXP = 13.0
OWN_ROWS = 112
HALO_ROWS = 64

f32 = jnp.float32
bf16 = jnp.bfloat16


def column_of(n):
    return 8 * (n % 128 - LEAD) + n // 128


def spread_table():
    columns = column_of(np.arange(1024))
    return (np.arange(896)[:, None] - 256 == columns[None, :]).astype(ml_dtypes.bfloat16)


def collect_table():
    columns = column_of(np.arange(1024))
    return (columns[:, None] == np.arange(384)[None, :]).astype(ml_dtypes.bfloat16)


def centre(level):
    return 4.0 + 4.0**level * 0.25 / (CLAT * CLAT)


def west(v, hop):
    first = pltpu.roll(v[-1], hop, 1)[None]
    return jnp.concatenate([first, v[:-1]], 0) if v.shape[0] > 1 else first


def east(v, hop):
    last = pltpu.roll(v[0], 128 - hop, 1)[None]
    return jnp.concatenate([v[1:], last], 0) if v.shape[0] > 1 else last


def above_first(v):
    lanes = lax.broadcasted_iota(jnp.int32, (8, 128), 0)
    return jnp.stack([jnp.where(lanes > 0, pltpu.roll(v[p], 1, 0), 0.0) for p in range(v.shape[0])])


def below_last(v):
    lanes = lax.broadcasted_iota(jnp.int32, (8, 128), 0)
    return jnp.stack([jnp.where(lanes < 7, pltpu.roll(v[p], 7, 0), 0.0) for p in range(v.shape[0])])


def doubled(v, phases):
    if v.shape[0] == phases:
        return v
    return jnp.concatenate([v[p // 2][None] for p in range(phases)], 0)


def loop(count, body, carry, unroll):
    if unroll >= count:
        for step in range(count):
            carry = body(step, carry)
        return carry
    return lax.fori_loop(0, count, body, carry, unroll=unroll)


def shape_of(level):
    return ROWS >> level, max(PHASES >> level, 1), (2 if level == GRIDS - 1 else 1)


UNROLL = (16, 16, 8, 4, 2)


def sweep(level, x, b, start=False, coarse=None):
    rows, phases, hop = shape_of(level)
    gain = OMEGA / centre(level)
    if start:
        old = lambda r, s: b[r]
    elif coarse is not None:
        old = lambda r, s: x[r] + doubled(coarse[s], phases)
    else:
        old = lambda r, s: x[r]
    first = old(0, 0)
    top = above_first(old(rows - 1, rows // 2 - 1))
    if not start:
        x[rows] = below_last(first)

    def step(r, above, here, below):
        near = (above + below) + (west(here, hop) + east(here, hop))
        if start:
            return (1.2 * gain) * here + (gain * gain) * near
        return 0.2 * here + gain * (b[r] + near)

    def body(s, carry):
        prev, c0 = carry
        c1 = old(2 * s + 1, s)
        n = old(2 * s + 2, s + 1)
        x[2 * s] = step(2 * s, prev, c0, c1)
        x[2 * s + 1] = step(2 * s + 1, c0, c1, n)
        return c1, n

    loop(rows // 2, body, (top, first), UNROLL[level])


def residual(level, x, b, out):
    rows, phases, hop = shape_of(level)
    weight = 2.0 - centre(level)
    first = x[0]
    top = above_first(x[rows - 1])
    x[rows] = below_last(first)
    lane = lax.broadcasted_iota(jnp.int32, (8, 128), 1)

    def across(v):
        if phases > 1:
            return jnp.concatenate([(v[2 * p] + v[2 * p + 1])[None] for p in range(phases // 2)], 0)
        return v + jnp.where(lane % 2 == 0, pltpu.roll(v[0], 127, 1), pltpu.roll(v[0], 1, 1))[None]

    def sides(v):
        if phases > 1:
            to_west = jnp.concatenate([pltpu.roll(v[-1], 1, 1)[None]] + [v[2 * p - 1][None] for p in range(1, phases // 2)], 0)
            to_east = jnp.concatenate([v[2 * p][None] for p in range(1, phases // 2)] + [pltpu.roll(v[0], 127, 1)[None]], 0)
            return to_west + to_east
        near = jnp.where(lane % 2 == 0, pltpu.roll(v[0], 1, 1), pltpu.roll(v[0], 127, 1))
        far = jnp.where(lane % 2 == 0, pltpu.roll(v[0], 126, 1), pltpu.roll(v[0], 2, 1))
        return (near + far)[None]

    def body(s, carry):
        prev, c0 = carry
        c1 = x[2 * s + 1]
        n = x[2 * s + 2]
        flat_n = across(n)
        pair = c0 + c1
        out[s] = across(b[2 * s] + b[2 * s + 1]) + weight * across(pair) + ((prev + flat_n) + sides(pair))
        return across(c1), n

    loop(rows // 2, body, (across(top), first), UNROLL[level])
    out[rows // 2] = below_last(out[0])


def vcycle(level, x, b, fresh):
    rows = shape_of(level)[0]
    if level == GRIDS - 1:
        sweep(level, x[level], b[level], start=True)
        sweep(level, x[level], b[level])
    else:
        if fresh:
            sweep(level, x[level], b[level], start=True)
        else:
            sweep(level, x[level], b[level])
            sweep(level, x[level], b[level])
        residual(level, x[level], b[level], b[level + 1])
        vcycle(level + 1, x, b, True)
        sweep(level, x[level], b[level], coarse=x[level + 1])
    sweep(level, x[level], b[level])
    if level > 0:
        x[level][rows] = jnp.zeros(x[level].shape[1:], f32)


def hat(position, index):
    return jnp.maximum(1.0 - jnp.abs(position - index), 0.0)


def own_number(ref, height, at, lane):
    return [ref[pl.ds(height * half + at, 8, stride=2 * height), :][:, lane : lane + 1] for half in range(2)]


def spread_rows(split, sources, width):
    slot = lax.broadcasted_iota(jnp.int32, (8, 128), 1) // 32

    def put(j, s, pair):
        block = jnp.concatenate(pair, 0)
        high = block.astype(bf16)
        split[16 * s : 16 * s + 16, 128 * j : 128 * j + 128] = high
        split[16 * s : 16 * s + 16, width + 128 * j : width + 128 * j + 128] = (block - high.astype(f32)).astype(bf16)

    for j, (ref, height, units, number, outer) in enumerate(sources):
        scale = [jnp.exp2(k - IN_EXP) for k in own_number(ref, height, *number)]
        for half in range(2):
            rows = {}
            for a in range(16):
                get = lambda at: ref[pl.ds(height * half + at + a, 8, stride=2 * height), :] * scale[half]
                if outer:
                    one, two = get(units[0]), get(units[1])
                    rows[a] = jnp.where(slot % 2 == 0, one, two)
                    rows[a + 16] = jnp.where(slot % 2 == 0, two, one)
                else:
                    middle = get(units[1])
                    low = jnp.where((slot == 1) | (slot == 2), middle, 0.0)
                    high = jnp.where(slot == 1, pltpu.roll(middle, 32, 1), jnp.where(slot == 2, pltpu.roll(middle, 96, 1), 0.0))
                    if units[0] is not None:
                        one = get(units[0])
                        low = jnp.where(slot == 0, one, low)
                        high = jnp.where(slot == 0, pltpu.roll(one, 96, 1), high)
                    if units[2] is not None:
                        two = get(units[2])
                        low = jnp.where(slot == 3, two, low)
                        high = jnp.where(slot == 3, pltpu.roll(two, 32, 1), high)
                    rows[a] = low
                    rows[a + 16] = high
            for s in range(16):
                put(j, 16 * half + s, (rows[2 * s], rows[2 * s + 1]))


OWN_NUMBER = (32, 127)
RIGHT_NUMBER = (32, 127)
LEFT_NUMBER = (16, 2)


def row_winds(row_table, low, high):
    lane = lax.broadcasted_iota(jnp.int32, (8, 128), 1)
    both = []
    for offset in (0, 8):
        rows = []
        for i in range(16):
            parts = []
            for ref, height, at, number in (low, high):
                first = i * height + at
                number_row = i * height + number[0]
                scale = jnp.exp2(ref[number_row : number_row + 1, number[1] : number[1] + 1] - IN_EXP)
                parts.append(ref[first + offset : first + offset + 8, :] * scale)
            rows.append(jnp.where(lane < 64, parts[0], parts[1]))
        both.append(jnp.concatenate(rows, 0))
    table = jnp.concatenate(both, 1).astype(bf16)
    return jnp.dot(row_table, table, preferred_element_type=f32).astype(bf16)


def own_kernel(own, spread, force0, row_table, winds, split):
    spread_rows(
        split,
        (
            (own, OWN_ROWS, (0, 16), OWN_NUMBER, True),
            (own, OWN_ROWS, (32, 48, 64), OWN_NUMBER, False),
            (own, OWN_ROWS, (80, 96), OWN_NUMBER, True),
        ),
        384,
    )
    force0[...] = jnp.dot(split[:, 0:384], spread[...], preferred_element_type=f32) + jnp.dot(
        split[:, 384:768], spread[...], preferred_element_type=f32
    )
    lane = lax.broadcasted_iota(jnp.int32, (8, 128), 1).astype(f32)
    parts = []
    for first in own_number(own, OWN_ROWS, OWN_NUMBER[0], 125):
        for a in range(32):
            parts.append(hat(first + a * 0.25, lane))
    table = jnp.concatenate(parts, 0).astype(bf16)
    row_table[...] = table
    winds[...] = row_winds(table, (own, OWN_ROWS, 64, OWN_NUMBER), (own, OWN_ROWS, 32, OWN_NUMBER))


def kernel(own, left, right, spread, collect, force0, row_table, winds, out, bound, x0, x1, x2, x3, x4, b0, b1, b2, b3, b4, gx, gy, split, flat):
    x = (x0, x1, x2, x3, x4)
    b = (b0, b1, b2, b3, b4)
    spread_rows(
        split,
        (
            (left, HALO_ROWS, (None, 0, 16), LEFT_NUMBER, False),
            (left, HALO_ROWS, (32, 48), LEFT_NUMBER, True),
            (right, HALO_ROWS, (0, 16), RIGHT_NUMBER, True),
            (right, HALO_ROWS, (32, 48, None), RIGHT_NUMBER, False),
        ),
        512,
    )
    n = lax.broadcasted_iota(jnp.int32, (1, 1024), 1)
    column = 8 * ((n & 127) - LEAD) + (n >> 7)

    def shift_of(ref, at, lane):
        first = ref[at : at + 1, lane : lane + 1]
        return first - 96.0 * jnp.floor((first + 48.0) * (1.0 / 96.0))

    shifts = (shift_of(left, 16, 1), shift_of(own, 32, 126), shift_of(right, 32, 126))

    def place(c):
        return c.astype(f32) * 0.25 + 96.0 + jnp.where(c < 0, shifts[0], jnp.where(c < 384, shifts[1], shifts[2]))

    m = lax.broadcasted_iota(jnp.int32, (256, 1), 0)
    lane = m & 127
    spot = jnp.where(lane < 64, lane + 32, lane - 64) + jnp.where(m < 128, 96, jnp.where(lane < 64, 0, 192))
    void = (lane >= 125) | (lane < jnp.where(m < 128, 29, 3))
    index = jnp.where(void, -100000, spot).astype(f32)
    slope = (2.0 * (hat(place(column + 1), index) - hat(place(column - 1), index))).astype(bf16)
    value = (2.0 * hat(place(column), index)).astype(bf16)
    sides = row_winds(row_table[...], (left, HALO_ROWS, 16, LEFT_NUMBER), (right, HALO_ROWS, 32, RIGHT_NUMBER))
    wx = jnp.concatenate([winds[:, 0:128], sides[:, 0:128]], 1)
    wy = jnp.concatenate([winds[:, 128:256], sides[:, 128:256]], 1)
    gx[...] = (
        jnp.dot(split[0:512, 0:512], spread[...], preferred_element_type=f32)
        + jnp.dot(split[0:512, 512:1024], spread[...], preferred_element_type=f32)
        + jnp.dot(wx, slope, preferred_element_type=f32)
    )
    gy[...] = jnp.dot(wy, value, preferred_element_type=f32)

    def cut(ref, r):
        return jnp.stack([ref[8 * r : 8 * r + 8, 128 * p : 128 * p + 128] for p in range(PHASES)])

    first = cut(gy, 0)
    above, here = above_first(cut(gy, ROWS - 1)), first
    for r in range(ROWS):
        below = cut(gy, r + 1) if r < ROWS - 1 else below_last(first)
        b0[r] = cut(force0, r) + cut(gx, r) + (below - above)
        above, here = here, below
    b0[ROWS] = below_last(b0[0])

    for cycle in range(CYCLES):
        vcycle(0, x, b, cycle == 0)

    powers = own_number(own, OWN_ROWS, *OWN_NUMBER) + own_number(left, HALO_ROWS, *LEFT_NUMBER) + own_number(right, HALO_ROWS, *RIGHT_NUMBER)
    power = jnp.max(functools.reduce(jnp.maximum, powers), axis=0, keepdims=True) + (GAIN_EXP - IN_EXP)
    bound[...] = jnp.broadcast_to(jnp.exp2(power), (512, 384))
    scale = jnp.exp2(-power)
    for s in range(ROWS // 2):
        pair = jnp.concatenate([x0[2 * s], x0[2 * s + 1]], 1) * scale
        high = pair.astype(bf16)
        low = (pair - high.astype(f32)).astype(bf16)
        for p in range(PHASES):
            split[16 * s : 16 * s + 16, 128 * p : 128 * p + 128] = high[p]
            split[512 + 16 * s : 528 + 16 * s, 128 * p : 128 * p + 128] = low[p]
    block = jnp.dot(split[0:512, :], collect[...], preferred_element_type=f32) + jnp.dot(
        split[512:1024, :], collect[...], preferred_element_type=f32
    )
    for j in range(3):
        for r in range(ROWS):
            flat[pl.ds(512 * j + r, 8, stride=64), :] = block[8 * r : 8 * r + 8, 128 * j : 128 * j + 128]
    for j in range(3):
        out[:, 128 * j : 128 * j + 128] = flat[512 * j : 512 * j + 512, :]


PARAMS = dict(compiler_params=pltpu.CompilerParams(vmem_limit_bytes=40 * 1024 * 1024))


def core_own(own, interpret=False):
    return pl.pallas_call(
        own_kernel,
        out_shape=(
            jax.ShapeDtypeStruct((512, 1024), f32),
            jax.ShapeDtypeStruct((512, 128), bf16),
            jax.ShapeDtypeStruct((512, 256), bf16),
        ),
        scratch_shapes=[pltpu.VMEM((512, 768), bf16)],
        interpret=interpret,
        **PARAMS,
    )(own, jnp.asarray(spread_table()[256:640]))


def core(own, left, right, parts, interpret=False):
    grids = []
    for level in range(GRIDS):
        rows, phases, _ = shape_of(level)
        grids.append(pltpu.VMEM((rows + 1, phases, 8, 128), f32))
    table = spread_table()
    return pl.pallas_call(
        kernel,
        out_shape=(jax.ShapeDtypeStruct((512, 384), f32), jax.ShapeDtypeStruct((512, 384), f32)),
        scratch_shapes=grids
        + grids
        + [
            pltpu.VMEM((512, 1024), f32),
            pltpu.VMEM((512, 1024), f32),
            pltpu.VMEM((1024, 1024), bf16),
            pltpu.VMEM((1536, 128), f32),
        ],
        interpret=interpret,
        **PARAMS,
    )(own, left, right, jnp.asarray(np.concatenate([table[0:256], table[640:896]])), jnp.asarray(collect_table()), *parts)


def parcel_kernel(lat_first, lon_first, increments_hbm, winds_hbm, out, increments, ens_winds, sems):
    copies = [
        pltpu.make_async_copy(increments_hbm, increments, sems.at[0]),
        pltpu.make_async_copy(winds_hbm, ens_winds, sems.at[1]),
    ]
    for copy in copies:
        copy.start()
    for copy in copies:
        copy.wait()
    top = jnp.max(jnp.max(jnp.abs(increments[...]), axis=(0, 1)), axis=(0, 1), keepdims=True)
    gust = jnp.max(jnp.max(jnp.abs(ens_winds[...].astype(f32)), axis=(0, 1)), axis=(0, 1), keepdims=True)
    top = jnp.maximum(jnp.maximum(top, 8.0 * gust), 1e-30)
    power = jnp.ceil(jnp.log2(top))
    scale = jnp.exp2(IN_EXP - power)
    lat, lon = lat_first[0].astype(f32), lon_first[0].astype(f32)
    lane = lax.broadcasted_iota(jnp.int32, (16, 128), 1)
    slot = lane // 32
    even = slot % 2 == 0
    for field in range(2):
        for k in range(8):
            d = 8 * field + k
            block = increments[field, k] * scale
            low, high = block[0:16], block[16:32]
            for at, c in ((0, 0), (80, 256)):
                out[d, at : at + 16, :] = jnp.where(even, low[:, c : c + 128], high[:, c : c + 128])
                out[d, at + 16 : at + 32, :] = jnp.where(even, high[:, c : c + 128], low[:, c : c + 128])
            low, high = low[:, 128:256], high[:, 128:256]
            on, back = pltpu.roll(high, 32, 1), pltpu.roll(high, 96, 1)
            u, v = ens_winds[0, k].astype(f32) * scale, ens_winds[1, k].astype(f32) * scale
            across, along = (v, -u) if field == 0 else (u, v)
            winds = jnp.concatenate([across, along], 0)
            winds = jnp.concatenate([winds, jnp.zeros((16, 32), f32)], 1)
            first = jnp.where(slot == 0, low, jnp.where(slot == 1, on, pltpu.roll(winds, 64, 1)))
            first = jnp.where(lane == 125, lat, jnp.where(lane == 126, lon, jnp.where(lane == 127, power, first)))
            last = jnp.where(slot == 3, low, jnp.where(slot == 2, back, pltpu.roll(winds, 96, 1)))
            last = jnp.where(lane == 0, lat, jnp.where(lane == 1, lon, jnp.where(lane == 2, power, last)))
            out[d, 32:48, :] = first
            out[d, 48:64, :] = jnp.where(slot == 0, back, jnp.where(slot == 3, on, low))
            out[d, 64:80, :] = last


def in_hbm(value):
    return pltpu.with_memory_space_constraint(value, pltpu.HBM)


def parcel(increments, ens_winds, lat_offsets, lon_offsets, interpret=False):
    scalar = pl.BlockSpec(memory_space=pltpu.SMEM)
    whole = pl.BlockSpec(memory_space=pltpu.HBM)
    return pl.pallas_call(
        parcel_kernel,
        out_shape=jax.ShapeDtypeStruct((16, OWN_ROWS, 128), f32),
        in_specs=[scalar, scalar, whole, whole],
        scratch_shapes=[
            pltpu.VMEM(increments.shape, f32),
            pltpu.VMEM(ens_winds.shape, bf16),
            pltpu.SemaphoreType.DMA((2,)),
        ],
        interpret=interpret,
        **PARAMS,
    )(lat_offsets, lon_offsets, in_hbm(increments), in_hbm(ens_winds))


def local(increments, ens_winds, lat_offsets, lon_offsets):
    count = lax.axis_size("lon")
    mine = parcel(increments, ens_winds, lat_offsets, lon_offsets).astype(jnp.float16)
    held, me = lax.optimization_barrier((lax.all_to_all(mine, "lat", 0, 0, tiled=True), lax.axis_index("lon")))
    even = me % 2 == 0
    to_left, to_right = held[:, 0:HALO_ROWS], held[:, OWN_ROWS - HALO_ROWS :]
    pairs0 = [(i, i ^ 1) for i in range(count)]
    pairs1 = [(i, (((i - 1) ^ 1) + 1) % count) for i in range(count)]
    got0 = lax.ppermute(jnp.where(even, to_right, to_left), "lon", pairs0)
    got1 = lax.ppermute(jnp.where(even, to_left, to_right), "lon", pairs1)
    own = held.astype(f32).reshape(16 * OWN_ROWS, 128)
    parts = core_own(own)
    left = jnp.where(even, got1, got0).astype(f32).reshape(16 * HALO_ROWS, 128)
    right = jnp.where(even, got0, got1).astype(f32).reshape(16 * HALO_ROWS, 128)
    done, bound = core(own, left, right, parts)
    back = lax.all_to_all(done.astype(jnp.float16).reshape(16, 32, 384), "lat", 0, 0, tiled=True)
    return (back.astype(f32) * bound.reshape(back.shape)).reshape(increments.shape)


def solution(mesh):
    in_specs = (P(None, None, "lat", "lon"), P(None, None, "lat", "lon"), P("lat"), P("lon"))
    out_specs = P(None, None, "lat", "lon")
    return jax.shard_map(local, mesh=mesh, in_specs=in_specs, out_specs=out_specs, check_vma=False)
```

```python
import functools

import jax
import jax.numpy as jnp
import ml_dtypes
import numpy as np
from jax import lax
from jax.experimental import pallas as pl
from jax.experimental.pallas import tpu as pltpu
from jax.sharding import PartitionSpec as P

CLAT = 32
GRIDS = 5
OMEGA = 0.8
COARSE_SWEEPS = 4
CYCLES = 2
ROWS = 64
PHASES = 8
LEAD = 40
IN_EXP = 14.0
GAIN_EXP = 13.0
OWN_ROWS = 112
HALO_ROWS = 64

f32 = jnp.float32
bf16 = jnp.bfloat16


def column_of(n):
    return 8 * (n % 128 - LEAD) + n // 128


def spread_table():
    columns = column_of(np.arange(1024))
    return (np.arange(896)[:, None] - 256 == columns[None, :]).astype(ml_dtypes.bfloat16)


def collect_table():
    n = np.arange(512)
    phase, lane = n // 128, n % 128
    second = (lane < 24) | (lane >= 104)
    columns = np.where(second, 8 * ((lane + 64) % 128 - LEAD) + phase + 4, 8 * (lane - LEAD) + phase)
    columns = np.where(second | ((lane >= LEAD) & (lane < LEAD + 48)), columns, -1)
    return (columns[:, None] == np.arange(384)[None, :]).astype(ml_dtypes.bfloat16)


def centre(level):
    return 4.0 + 4.0**level * 0.25 / (CLAT * CLAT)


def west(v, hop):
    first = pltpu.roll(v[-1], hop, 1)[None]
    return jnp.concatenate([first, v[:-1]], 0) if v.shape[0] > 1 else first


def east(v, hop):
    last = pltpu.roll(v[0], 128 - hop, 1)[None]
    return jnp.concatenate([v[1:], last], 0) if v.shape[0] > 1 else last


def above_first(v):
    lanes = lax.broadcasted_iota(jnp.int32, (8, 128), 0)
    return jnp.stack([jnp.where(lanes > 0, pltpu.roll(v[p], 1, 0), 0.0) for p in range(v.shape[0])])


def below_last(v):
    lanes = lax.broadcasted_iota(jnp.int32, (8, 128), 0)
    return jnp.stack([jnp.where(lanes < 7, pltpu.roll(v[p], 7, 0), 0.0) for p in range(v.shape[0])])


def doubled(v, phases):
    if v.shape[0] == phases:
        return v
    return jnp.concatenate([v[p // 2][None] for p in range(phases)], 0)


def loop(count, body, carry, unroll):
    if unroll >= count:
        for step in range(count):
            carry = body(step, carry)
        return carry
    return lax.fori_loop(0, count, body, carry, unroll=unroll)


def shape_of(level):
    return ROWS >> level, max(PHASES >> level, 1), (2 if level == GRIDS - 1 else 1)


UNROLL = (32, 16, 8, 4, 2)


def sweep(level, x, b, start=False, coarse=None):
    rows, phases, hop = shape_of(level)
    gain = OMEGA / centre(level)
    if start:
        old = lambda r, s: b[r]
    elif coarse is not None:
        old = lambda r, s: x[r] + doubled(coarse[s], phases)
    else:
        old = lambda r, s: x[r]
    first = old(0, 0)
    top = above_first(old(rows - 1, rows // 2 - 1))
    if not start:
        x[rows] = below_last(first)

    def step(r, above, here, below):
        near = (above + below) + (west(here, hop) + east(here, hop))
        if start:
            return (1.2 * gain) * here + (gain * gain) * near
        return 0.2 * here + gain * (b[r] + near)

    def body(s, carry):
        prev, c0 = carry
        c1 = old(2 * s + 1, s)
        n = old(2 * s + 2, s + 1)
        x[2 * s] = step(2 * s, prev, c0, c1)
        x[2 * s + 1] = step(2 * s + 1, c0, c1, n)
        return c1, n

    loop(rows // 2, body, (top, first), UNROLL[level])


def residual(level, x, b, out):
    rows, phases, hop = shape_of(level)
    weight = 2.0 - centre(level)
    first = x[0]
    top = above_first(x[rows - 1])
    x[rows] = below_last(first)
    lane = lax.broadcasted_iota(jnp.int32, (8, 128), 1)

    def across(v):
        if phases > 1:
            return jnp.concatenate([(v[2 * p] + v[2 * p + 1])[None] for p in range(phases // 2)], 0)
        return v + jnp.where(lane % 2 == 0, pltpu.roll(v[0], 127, 1), pltpu.roll(v[0], 1, 1))[None]

    def sides(v):
        if phases > 1:
            to_west = jnp.concatenate([pltpu.roll(v[-1], 1, 1)[None]] + [v[2 * p - 1][None] for p in range(1, phases // 2)], 0)
            to_east = jnp.concatenate([v[2 * p][None] for p in range(1, phases // 2)] + [pltpu.roll(v[0], 127, 1)[None]], 0)
            return to_west + to_east
        near = jnp.where(lane % 2 == 0, pltpu.roll(v[0], 1, 1), pltpu.roll(v[0], 127, 1))
        far = jnp.where(lane % 2 == 0, pltpu.roll(v[0], 126, 1), pltpu.roll(v[0], 2, 1))
        return (near + far)[None]

    def body(s, carry):
        prev, c0 = carry
        c1 = x[2 * s + 1]
        n = x[2 * s + 2]
        flat_n = across(n)
        pair = c0 + c1
        out[s] = across(b[2 * s] + b[2 * s + 1]) + weight * across(pair) + ((prev + flat_n) + sides(pair))
        return across(c1), n

    loop(rows // 2, body, (across(top), first), UNROLL[level])
    out[rows // 2] = below_last(out[0])


def coarsest(x, b):
    level = GRIDS - 1
    rows, _, hop = shape_of(level)
    gain = OMEGA / centre(level)
    source = [b[r][0] for r in range(rows)]
    sub = lax.broadcasted_iota(jnp.int32, (8, 128), 0)
    v = source
    for turn in range(COARSE_SWEEPS - 1):
        above = [jnp.where(sub > 0, pltpu.roll(v[-1], 1, 0), 0.0)] + v[:-1]
        below = v[1:] + [jnp.where(sub < 7, pltpu.roll(v[0], 7, 0), 0.0)]
        near = [(above[r] + below[r]) + (pltpu.roll(v[r], hop, 1) + pltpu.roll(v[r], 128 - hop, 1)) for r in range(rows)]
        if turn == 0:
            v = [(1.2 * gain) * v[r] + (gain * gain) * near[r] for r in range(rows)]
        else:
            v = [0.2 * v[r] + gain * (source[r] + near[r]) for r in range(rows)]
    for r in range(rows):
        x[r] = v[r][None]
    x[rows] = jnp.zeros(x.shape[1:], f32)


def vcycle(level, x, b, fresh):
    if level == GRIDS - 1:
        coarsest(x[level], b[level])
        return
    if fresh:
        sweep(level, x[level], b[level], start=True)
    else:
        sweep(level, x[level], b[level])
        sweep(level, x[level], b[level])
    residual(level, x[level], b[level], b[level + 1])
    vcycle(level + 1, x, b, True)
    sweep(level, x[level], b[level], coarse=x[level + 1])
    sweep(level, x[level], b[level])
    if level > 0:
        x[level][shape_of(level)[0]] = jnp.zeros(x[level].shape[1:], f32)


def hat(position, index):
    return jnp.maximum(1.0 - jnp.abs(position - index), 0.0)


def own_number(ref, height, at, lane):
    return [ref[pl.ds(height * half + at, 8, stride=2 * height), :][:, lane : lane + 1] for half in range(2)]


def spread_rows(split, sources, width):
    slot = lax.broadcasted_iota(jnp.int32, (8, 128), 1) // 32

    def put(j, s, pair):
        block = jnp.concatenate(pair, 0)
        high = block.astype(bf16)
        split[16 * s : 16 * s + 16, 128 * j : 128 * j + 128] = high
        split[16 * s : 16 * s + 16, width + 128 * j : width + 128 * j + 128] = (block - high.astype(f32)).astype(bf16)

    for j, (ref, height, units, number, outer) in enumerate(sources):
        scale = [jnp.exp2(k - IN_EXP) for k in own_number(ref, height, *number)]
        for half in range(2):
            rows = {}
            for a in range(16):
                get = lambda at: ref[pl.ds(height * half + at + a, 8, stride=2 * height), :] * scale[half]
                if outer:
                    one, two = get(units[0]), get(units[1])
                    rows[a] = jnp.where(slot % 2 == 0, one, two)
                    rows[a + 16] = jnp.where(slot % 2 == 0, two, one)
                else:
                    middle = get(units[1])
                    low = jnp.where((slot == 1) | (slot == 2), middle, 0.0)
                    high = jnp.where(slot == 1, pltpu.roll(middle, 32, 1), jnp.where(slot == 2, pltpu.roll(middle, 96, 1), 0.0))
                    if units[0] is not None:
                        one = get(units[0])
                        low = jnp.where(slot == 0, one, low)
                        high = jnp.where(slot == 0, pltpu.roll(one, 96, 1), high)
                    if units[2] is not None:
                        two = get(units[2])
                        low = jnp.where(slot == 3, two, low)
                        high = jnp.where(slot == 3, pltpu.roll(two, 32, 1), high)
                    rows[a] = low
                    rows[a + 16] = high
            for s in range(16):
                put(j, 16 * half + s, (rows[2 * s], rows[2 * s + 1]))


OWN_NUMBER = (32, 127)
RIGHT_NUMBER = (32, 127)
LEFT_NUMBER = (16, 2)


def row_winds(row_table, low, high):
    lane = lax.broadcasted_iota(jnp.int32, (8, 128), 1)
    both = []
    for offset in (0, 8):
        rows = []
        for i in range(16):
            parts = []
            for ref, height, at, number in (low, high):
                first = i * height + at
                number_row = i * height + number[0]
                scale = jnp.exp2(ref[number_row : number_row + 1, number[1] : number[1] + 1] - IN_EXP)
                parts.append(ref[first + offset : first + offset + 8, :] * scale)
            rows.append(jnp.where(lane < 64, parts[0], parts[1]))
        both.append(jnp.concatenate(rows, 0))
    table = jnp.concatenate(both, 1).astype(bf16)
    return jnp.dot(row_table, table, preferred_element_type=f32).astype(bf16)


def own_kernel(own, spread, force0, row_table, winds, split):
    spread_rows(
        split,
        (
            (own, OWN_ROWS, (0, 16), OWN_NUMBER, True),
            (own, OWN_ROWS, (32, 48, 64), OWN_NUMBER, False),
            (own, OWN_ROWS, (80, 96), OWN_NUMBER, True),
        ),
        384,
    )
    force0[...] = jnp.dot(split[:, 0:384], spread[...], preferred_element_type=f32) + jnp.dot(
        split[:, 384:768], spread[...], preferred_element_type=f32
    )
    lane = lax.broadcasted_iota(jnp.int32, (8, 128), 1).astype(f32)
    parts = []
    for first in own_number(own, OWN_ROWS, OWN_NUMBER[0], 125):
        for a in range(32):
            parts.append(hat(first + a * 0.25, lane))
    table = jnp.concatenate(parts, 0).astype(bf16)
    row_table[...] = table
    winds[...] = row_winds(table, (own, OWN_ROWS, 64, OWN_NUMBER), (own, OWN_ROWS, 32, OWN_NUMBER))


def kernel(own, left, right, spread, collect, force0, row_table, winds, out, bound, x0, x1, x2, x3, x4, b0, b1, b2, b3, b4, gx, gy, split, flat):
    x = (x0, x1, x2, x3, x4)
    b = (b0, b1, b2, b3, b4)
    spread_rows(
        split,
        (
            (left, HALO_ROWS, (None, 0, 16), LEFT_NUMBER, False),
            (left, HALO_ROWS, (32, 48), LEFT_NUMBER, True),
            (right, HALO_ROWS, (0, 16), RIGHT_NUMBER, True),
            (right, HALO_ROWS, (32, 48, None), RIGHT_NUMBER, False),
        ),
        512,
    )
    n = lax.broadcasted_iota(jnp.int32, (1, 1024), 1)
    column = 8 * ((n & 127) - LEAD) + (n >> 7)

    def shift_of(ref, at, lane):
        first = ref[at : at + 1, lane : lane + 1]
        return first - 96.0 * jnp.floor((first + 48.0) * (1.0 / 96.0))

    shifts = (shift_of(left, 16, 1), shift_of(own, 32, 126), shift_of(right, 32, 126))

    def place(c):
        return c.astype(f32) * 0.25 + 96.0 + jnp.where(c < 0, shifts[0], jnp.where(c < 384, shifts[1], shifts[2]))

    m = lax.broadcasted_iota(jnp.int32, (256, 1), 0)
    lane = m & 127
    spot = jnp.where(lane < 64, lane + 32, lane - 64) + jnp.where(m < 128, 96, jnp.where(lane < 64, 0, 192))
    void = (lane >= 125) | (lane < jnp.where(m < 128, 29, 3))
    index = jnp.where(void, -100000, spot).astype(f32)
    slope = (2.0 * (hat(place(column + 1), index) - hat(place(column - 1), index))).astype(bf16)
    value = (2.0 * hat(place(column), index)).astype(bf16)
    sides = row_winds(row_table[...], (left, HALO_ROWS, 16, LEFT_NUMBER), (right, HALO_ROWS, 32, RIGHT_NUMBER))
    wx = jnp.concatenate([winds[:, 0:128], sides[:, 0:128]], 1)
    wy = jnp.concatenate([winds[:, 128:256], sides[:, 128:256]], 1)
    gx[...] = (
        jnp.dot(split[:, 0:512], spread[...], preferred_element_type=f32)
        + jnp.dot(split[:, 512:1024], spread[...], preferred_element_type=f32)
        + jnp.dot(wx, slope, preferred_element_type=f32)
    )
    gy[...] = jnp.dot(wy, value, preferred_element_type=f32)

    def cut(ref, r):
        return jnp.stack([ref[8 * r : 8 * r + 8, 128 * p : 128 * p + 128] for p in range(PHASES)])

    first = cut(gy, 0)
    above, here = above_first(cut(gy, ROWS - 1)), first
    for r in range(ROWS):
        below = cut(gy, r + 1) if r < ROWS - 1 else below_last(first)
        b0[r] = cut(force0, r) + cut(gx, r) + (below - above)
        above, here = here, below
    b0[ROWS] = below_last(b0[0])

    for cycle in range(CYCLES):
        vcycle(0, x, b, cycle == 0)

    powers = own_number(own, OWN_ROWS, *OWN_NUMBER) + own_number(left, HALO_ROWS, *LEFT_NUMBER) + own_number(right, HALO_ROWS, *RIGHT_NUMBER)
    power = jnp.max(functools.reduce(jnp.maximum, powers), axis=0, keepdims=True) + (GAIN_EXP - IN_EXP)
    bound[...] = jnp.broadcast_to(jnp.exp2(power), (512, 384))
    scale = jnp.exp2(-power)
    lane = lax.broadcasted_iota(jnp.int32, (8, 128), 1)
    inside = (lane >= LEAD) & (lane < LEAD + 48)
    for s in range(ROWS // 2):
        for p in range(PHASES // 2):
            pair = [jnp.where(inside, x0[r, p], pltpu.roll(x0[r, p + 4], 64, 1)) for r in (2 * s, 2 * s + 1)]
            pair = jnp.concatenate(pair, 0) * scale
            high = pair.astype(bf16)
            split[16 * s : 16 * s + 16, 128 * p : 128 * p + 128] = high
            split[16 * s : 16 * s + 16, 512 + 128 * p : 640 + 128 * p] = (pair - high.astype(f32)).astype(bf16)
    block = jnp.dot(split[:, 0:512], collect[...], preferred_element_type=f32) + jnp.dot(
        split[:, 512:1024], collect[...], preferred_element_type=f32
    )
    for j in range(3):
        for r in range(ROWS):
            flat[pl.ds(512 * j + r, 8, stride=64), :] = block[8 * r : 8 * r + 8, 128 * j : 128 * j + 128]
    for j in range(3):
        out[:, 128 * j : 128 * j + 128] = flat[512 * j : 512 * j + 512, :]


PARAMS = dict(compiler_params=pltpu.CompilerParams(vmem_limit_bytes=40 * 1024 * 1024))


def core_own(own, interpret=False):
    return pl.pallas_call(
        own_kernel,
        out_shape=(
            jax.ShapeDtypeStruct((512, 1024), f32),
            jax.ShapeDtypeStruct((512, 128), bf16),
            jax.ShapeDtypeStruct((512, 256), bf16),
        ),
        scratch_shapes=[pltpu.VMEM((512, 768), bf16)],
        interpret=interpret,
        **PARAMS,
    )(own, jnp.asarray(spread_table()[256:640]))


def core(own, left, right, parts, interpret=False):
    grids = []
    for level in range(GRIDS):
        rows, phases, _ = shape_of(level)
        grids.append(pltpu.VMEM((rows + 1, phases, 8, 128), f32))
    table = spread_table()
    return pl.pallas_call(
        kernel,
        out_shape=(jax.ShapeDtypeStruct((512, 384), f32), jax.ShapeDtypeStruct((512, 384), f32)),
        scratch_shapes=grids
        + grids
        + [
            pltpu.VMEM((512, 1024), f32),
            pltpu.VMEM((512, 1024), f32),
            pltpu.VMEM((512, 1024), bf16),
            pltpu.VMEM((1536, 128), f32),
        ],
        interpret=interpret,
        **PARAMS,
    )(own, left, right, jnp.asarray(np.concatenate([table[0:256], table[640:896]])), jnp.asarray(collect_table()), *parts)


def parcel_kernel(lat_first, lon_first, increments_hbm, winds_hbm, out, odd, increments, ens_winds, sems):
    copies = [
        pltpu.make_async_copy(increments_hbm, increments, sems.at[0]),
        pltpu.make_async_copy(winds_hbm, ens_winds, sems.at[1]),
    ]
    for copy in copies:
        copy.start()
    for copy in copies:
        copy.wait()
    top = jnp.max(jnp.max(jnp.abs(increments[...]), axis=(0, 1)), axis=(0, 1), keepdims=True)
    gust = jnp.max(jnp.max(jnp.abs(ens_winds[...].astype(f32)), axis=(0, 1)), axis=(0, 1), keepdims=True)
    top = jnp.maximum(jnp.maximum(top, 8.0 * gust), 1e-30)
    power = jnp.ceil(jnp.log2(top))
    scale = jnp.exp2(IN_EXP - power)
    lat, lon = lat_first[0].astype(f32), lon_first[0].astype(f32)
    odd[...] = jnp.full(odd.shape, ((lon_first[0] + 48) // 96 % 2).astype(f32))
    lane = lax.broadcasted_iota(jnp.int32, (16, 128), 1)
    slot = lane // 32
    even = slot % 2 == 0
    for field in range(2):
        for k in range(8):
            d = 8 * field + k
            block = increments[field, k] * scale
            low, high = block[0:16], block[16:32]
            for at, c in ((0, 0), (80, 256)):
                out[d, at : at + 16, :] = jnp.where(even, low[:, c : c + 128], high[:, c : c + 128])
                out[d, at + 16 : at + 32, :] = jnp.where(even, high[:, c : c + 128], low[:, c : c + 128])
            low, high = low[:, 128:256], high[:, 128:256]
            on, back = pltpu.roll(high, 32, 1), pltpu.roll(high, 96, 1)
            u, v = ens_winds[0, k].astype(f32) * scale, ens_winds[1, k].astype(f32) * scale
            across, along = (v, -u) if field == 0 else (u, v)
            winds = jnp.concatenate([across, along], 0)
            winds = jnp.concatenate([winds, jnp.zeros((16, 32), f32)], 1)
            first = jnp.where(slot == 0, low, jnp.where(slot == 1, on, pltpu.roll(winds, 64, 1)))
            first = jnp.where(lane == 125, lat, jnp.where(lane == 126, lon, jnp.where(lane == 127, power, first)))
            last = jnp.where(slot == 3, low, jnp.where(slot == 2, back, pltpu.roll(winds, 96, 1)))
            last = jnp.where(lane == 0, lat, jnp.where(lane == 1, lon, jnp.where(lane == 2, power, last)))
            out[d, 32:48, :] = first
            out[d, 48:64, :] = jnp.where(slot == 0, back, jnp.where(slot == 3, on, low))
            out[d, 64:80, :] = last


def in_hbm(value):
    return pltpu.with_memory_space_constraint(value, pltpu.HBM)


def parcel(increments, ens_winds, lat_offsets, lon_offsets, interpret=False):
    scalar = pl.BlockSpec(memory_space=pltpu.SMEM)
    whole = pl.BlockSpec(memory_space=pltpu.HBM)
    return pl.pallas_call(
        parcel_kernel,
        out_shape=(
            jax.ShapeDtypeStruct((16, OWN_ROWS, 128), f32),
            jax.ShapeDtypeStruct((16, HALO_ROWS, 128), f32),
        ),
        in_specs=[scalar, scalar, whole, whole],
        scratch_shapes=[
            pltpu.VMEM(increments.shape, f32),
            pltpu.VMEM(ens_winds.shape, bf16),
            pltpu.SemaphoreType.DMA((2,)),
        ],
        interpret=interpret,
        **PARAMS,
    )(lat_offsets, lon_offsets, in_hbm(increments), in_hbm(ens_winds))


def local(increments, ens_winds, lat_offsets, lon_offsets):
    count = lax.axis_size("lon")
    mine, odd = parcel(increments, ens_winds, lat_offsets, lon_offsets)
    held = lax.all_to_all(mine.astype(jnp.float16), "lat", 0, 0, tiled=True)
    even = odd < 0.5
    to_left, to_right = held[:, 0:HALO_ROWS], held[:, OWN_ROWS - HALO_ROWS :]
    pairs0 = [(i, i ^ 1) for i in range(count)]
    pairs1 = [(i, (((i - 1) ^ 1) + 1) % count) for i in range(count)]
    got0 = lax.ppermute(jnp.where(even, to_right, to_left), "lon", pairs0)
    got1 = lax.ppermute(jnp.where(even, to_left, to_right), "lon", pairs1)
    own = held.astype(f32).reshape(16 * OWN_ROWS, 128)
    parts = core_own(own)
    left = jnp.where(even, got1, got0).astype(f32).reshape(16 * HALO_ROWS, 128)
    right = jnp.where(even, got0, got1).astype(f32).reshape(16 * HALO_ROWS, 128)
    done, bound = core(own, left, right, parts)
    back = lax.all_to_all(done.astype(jnp.float16).reshape(16, 32, 384), "lat", 0, 0, tiled=True)
    return (back.astype(f32) * bound.reshape(back.shape)).reshape(increments.shape)


def solution(mesh):
    in_specs = (P(None, None, "lat", "lon"), P(None, None, "lat", "lon"), P("lat"), P("lon"))
    out_specs = P(None, None, "lat", "lon")
    return jax.shard_map(local, mesh=mesh, in_specs=in_specs, out_specs=out_specs, check_vma=False)
```

```python
import functools

import jax
import jax.numpy as jnp
import ml_dtypes
import numpy as np
from jax import lax
from jax.experimental import pallas as pl
from jax.experimental.pallas import tpu as pltpu
from jax.sharding import PartitionSpec as P

CLAT = 32
GRIDS = 5
OMEGA = 0.8
COARSE_SWEEPS = 4
CYCLES = 2
ROWS = 64
PHASES = 8
LEAD = 40
IN_EXP = 14.0
GAIN_EXP = 13.0
OWN_ROWS = 112
HALO_ROWS = 64

f32 = jnp.float32
bf16 = jnp.bfloat16


def column_of(n):
    return 8 * (n % 128 - LEAD) + n // 128


def spread_table():
    columns = column_of(np.arange(1024))
    return (np.arange(896)[:, None] - 256 == columns[None, :]).astype(ml_dtypes.bfloat16)


def collect_table():
    n = np.arange(512)
    phase, lane = n // 128, n % 128
    second = (lane < 24) | (lane >= 104)
    columns = np.where(second, 8 * ((lane + 64) % 128 - LEAD) + phase + 4, 8 * (lane - LEAD) + phase)
    columns = np.where(second | ((lane >= LEAD) & (lane < LEAD + 48)), columns, -1)
    return (columns[:, None] == np.arange(384)[None, :]).astype(ml_dtypes.bfloat16)


def centre(level):
    return 4.0 + 4.0**level * 0.25 / (CLAT * CLAT)


def west(v, hop):
    first = pltpu.roll(v[-1], hop, 1)[None]
    return jnp.concatenate([first, v[:-1]], 0) if v.shape[0] > 1 else first


def east(v, hop):
    last = pltpu.roll(v[0], 128 - hop, 1)[None]
    return jnp.concatenate([v[1:], last], 0) if v.shape[0] > 1 else last


def above_first(v):
    lanes = lax.broadcasted_iota(jnp.int32, (8, 128), 0)
    return jnp.stack([jnp.where(lanes > 0, pltpu.roll(v[p], 1, 0), 0.0) for p in range(v.shape[0])])


def below_last(v):
    lanes = lax.broadcasted_iota(jnp.int32, (8, 128), 0)
    return jnp.stack([jnp.where(lanes < 7, pltpu.roll(v[p], 7, 0), 0.0) for p in range(v.shape[0])])


def doubled(v, phases):
    if v.shape[0] == phases:
        return v
    return jnp.concatenate([v[p // 2][None] for p in range(phases)], 0)


def loop(count, body, carry, unroll):
    if unroll >= count:
        for step in range(count):
            carry = body(step, carry)
        return carry
    return lax.fori_loop(0, count, body, carry, unroll=unroll)


def shape_of(level):
    return ROWS >> level, max(PHASES >> level, 1), (2 if level == GRIDS - 1 else 1)


UNROLL = (32, 16, 8, 4, 2)


def sweep(level, x, b, start=False, coarse=None):
    rows, phases, hop = shape_of(level)
    gain = OMEGA / centre(level)
    if start:
        old = lambda r, s: b[r]
    elif coarse is not None:
        old = lambda r, s: x[r] + doubled(coarse[s], phases)
    else:
        old = lambda r, s: x[r]
    first = old(0, 0)
    top = above_first(old(rows - 1, rows // 2 - 1))
    if not start:
        x[rows] = below_last(first)

    def step(r, above, here, below):
        near = (above + below) + (west(here, hop) + east(here, hop))
        if start:
            return (1.2 * gain) * here + (gain * gain) * near
        return 0.2 * here + gain * (b[r] + near)

    def body(s, carry):
        prev, c0 = carry
        c1 = old(2 * s + 1, s)
        n = old(2 * s + 2, s + 1)
        x[2 * s] = step(2 * s, prev, c0, c1)
        x[2 * s + 1] = step(2 * s + 1, c0, c1, n)
        return c1, n

    loop(rows // 2, body, (top, first), UNROLL[level])


def residual(level, x, b, out):
    rows, phases, hop = shape_of(level)
    weight = 2.0 - centre(level)
    first = x[0]
    top = above_first(x[rows - 1])
    x[rows] = below_last(first)
    lane = lax.broadcasted_iota(jnp.int32, (8, 128), 1)

    def across(v):
        if phases > 1:
            return jnp.concatenate([(v[2 * p] + v[2 * p + 1])[None] for p in range(phases // 2)], 0)
        return v + jnp.where(lane % 2 == 0, pltpu.roll(v[0], 127, 1), pltpu.roll(v[0], 1, 1))[None]

    def sides(v):
        if phases > 1:
            to_west = jnp.concatenate([pltpu.roll(v[-1], 1, 1)[None]] + [v[2 * p - 1][None] for p in range(1, phases // 2)], 0)
            to_east = jnp.concatenate([v[2 * p][None] for p in range(1, phases // 2)] + [pltpu.roll(v[0], 127, 1)[None]], 0)
            return to_west + to_east
        near = jnp.where(lane % 2 == 0, pltpu.roll(v[0], 1, 1), pltpu.roll(v[0], 127, 1))
        far = jnp.where(lane % 2 == 0, pltpu.roll(v[0], 126, 1), pltpu.roll(v[0], 2, 1))
        return (near + far)[None]

    def body(s, carry):
        prev, c0 = carry
        c1 = x[2 * s + 1]
        n = x[2 * s + 2]
        flat_n = across(n)
        pair = c0 + c1
        out[s] = across(b[2 * s] + b[2 * s + 1]) + weight * across(pair) + ((prev + flat_n) + sides(pair))
        return across(c1), n

    loop(rows // 2, body, (across(top), first), UNROLL[level])
    out[rows // 2] = below_last(out[0])


def coarsest(x, b):
    level = GRIDS - 1
    rows, _, hop = shape_of(level)
    gain = OMEGA / centre(level)
    source = [b[r][0] for r in range(rows)]
    sub = lax.broadcasted_iota(jnp.int32, (8, 128), 0)
    v = source
    for turn in range(COARSE_SWEEPS - 1):
        above = [jnp.where(sub > 0, pltpu.roll(v[-1], 1, 0), 0.0)] + v[:-1]
        below = v[1:] + [jnp.where(sub < 7, pltpu.roll(v[0], 7, 0), 0.0)]
        near = [(above[r] + below[r]) + (pltpu.roll(v[r], hop, 1) + pltpu.roll(v[r], 128 - hop, 1)) for r in range(rows)]
        if turn == 0:
            v = [(1.2 * gain) * v[r] + (gain * gain) * near[r] for r in range(rows)]
        else:
            v = [0.2 * v[r] + gain * (source[r] + near[r]) for r in range(rows)]
    for r in range(rows):
        x[r] = v[r][None]
    x[rows] = jnp.zeros(x.shape[1:], f32)


def vcycle(level, x, b, fresh):
    if level == GRIDS - 1:
        coarsest(x[level], b[level])
        return
    if fresh:
        sweep(level, x[level], b[level], start=True)
    else:
        sweep(level, x[level], b[level])
        sweep(level, x[level], b[level])
    residual(level, x[level], b[level], b[level + 1])
    vcycle(level + 1, x, b, True)
    sweep(level, x[level], b[level], coarse=x[level + 1])
    sweep(level, x[level], b[level])
    if level > 0:
        x[level][shape_of(level)[0]] = jnp.zeros(x[level].shape[1:], f32)


def hat(position, index):
    return jnp.maximum(1.0 - jnp.abs(position - index), 0.0)


def own_number(ref, height, at, lane):
    return [ref[pl.ds(height * half + at, 8, stride=2 * height), :][:, lane : lane + 1] for half in range(2)]


def spread_rows(split, sources, width):
    slot = lax.broadcasted_iota(jnp.int32, (8, 128), 1) // 32

    def put(j, s, pair):
        block = jnp.concatenate(pair, 0)
        high = block.astype(bf16)
        split[16 * s : 16 * s + 16, 128 * j : 128 * j + 128] = high
        split[16 * s : 16 * s + 16, width + 128 * j : width + 128 * j + 128] = (block - high.astype(f32)).astype(bf16)

    for j, (ref, height, units, number, outer) in enumerate(sources):
        scale = [jnp.exp2(k - IN_EXP) for k in own_number(ref, height, *number)]
        for half in range(2):
            rows = {}
            for a in range(16):
                get = lambda at: ref[pl.ds(height * half + at + a, 8, stride=2 * height), :] * scale[half]
                if outer:
                    one, two = get(units[0]), get(units[1])
                    rows[a] = jnp.where(slot % 2 == 0, one, two)
                    rows[a + 16] = jnp.where(slot % 2 == 0, two, one)
                else:
                    middle = get(units[1])
                    low = jnp.where((slot == 1) | (slot == 2), middle, 0.0)
                    high = jnp.where(slot == 1, pltpu.roll(middle, 32, 1), jnp.where(slot == 2, pltpu.roll(middle, 96, 1), 0.0))
                    if units[0] is not None:
                        one = get(units[0])
                        low = jnp.where(slot == 0, one, low)
                        high = jnp.where(slot == 0, pltpu.roll(one, 96, 1), high)
                    if units[2] is not None:
                        two = get(units[2])
                        low = jnp.where(slot == 3, two, low)
                        high = jnp.where(slot == 3, pltpu.roll(two, 32, 1), high)
                    rows[a] = low
                    rows[a + 16] = high
            for s in range(16):
                put(j, 16 * half + s, (rows[2 * s], rows[2 * s + 1]))


OWN_NUMBER = (32, 127)
RIGHT_NUMBER = (32, 127)
LEFT_NUMBER = (16, 2)


def row_winds(row_table, low, high):
    lane = lax.broadcasted_iota(jnp.int32, (8, 128), 1)
    both = []
    for offset in (0, 8):
        rows = []
        for i in range(16):
            parts = []
            for ref, height, at, number in (low, high):
                first = i * height + at
                number_row = i * height + number[0]
                scale = jnp.exp2(ref[number_row : number_row + 1, number[1] : number[1] + 1] - IN_EXP)
                parts.append(ref[first + offset : first + offset + 8, :] * scale)
            rows.append(jnp.where(lane < 64, parts[0], parts[1]))
        both.append(jnp.concatenate(rows, 0))
    table = jnp.concatenate(both, 1).astype(bf16)
    return jnp.dot(row_table, table, preferred_element_type=f32).astype(bf16)


def own_kernel(own, spread, force0, row_table, winds, split):
    spread_rows(
        split,
        (
            (own, OWN_ROWS, (0, 16), OWN_NUMBER, True),
            (own, OWN_ROWS, (32, 48, 64), OWN_NUMBER, False),
            (own, OWN_ROWS, (80, 96), OWN_NUMBER, True),
        ),
        384,
    )
    force0[...] = jnp.dot(split[:, 0:384], spread[...], preferred_element_type=f32) + jnp.dot(
        split[:, 384:768], spread[...], preferred_element_type=f32
    )
    lane = lax.broadcasted_iota(jnp.int32, (8, 128), 1).astype(f32)
    parts = []
    for first in own_number(own, OWN_ROWS, OWN_NUMBER[0], 125):
        for a in range(32):
            parts.append(hat(first + a * 0.25, lane))
    table = jnp.concatenate(parts, 0).astype(bf16)
    row_table[...] = table
    winds[...] = row_winds(table, (own, OWN_ROWS, 64, OWN_NUMBER), (own, OWN_ROWS, 32, OWN_NUMBER))


def kernel(own, left, right, spread, collect, force0, row_table, winds, out, bound, x0, x1, x2, x3, x4, b0, b1, b2, b3, b4, gx, gy, split, flat):
    x = (x0, x1, x2, x3, x4)
    b = (b0, b1, b2, b3, b4)
    spread_rows(
        split,
        (
            (left, HALO_ROWS, (None, 0, 16), LEFT_NUMBER, False),
            (left, HALO_ROWS, (32, 48), LEFT_NUMBER, True),
            (right, HALO_ROWS, (0, 16), RIGHT_NUMBER, True),
            (right, HALO_ROWS, (32, 48, None), RIGHT_NUMBER, False),
        ),
        512,
    )
    n = lax.broadcasted_iota(jnp.int32, (1, 1024), 1)
    column = 8 * ((n & 127) - LEAD) + (n >> 7)

    def shift_of(ref, at, lane):
        first = ref[at : at + 1, lane : lane + 1]
        return first - 96.0 * jnp.floor((first + 48.0) * (1.0 / 96.0))

    shifts = (shift_of(left, 16, 1), shift_of(own, 32, 126), shift_of(right, 32, 126))

    def place(c):
        return c.astype(f32) * 0.25 + 96.0 + jnp.where(c < 0, shifts[0], jnp.where(c < 384, shifts[1], shifts[2]))

    m = lax.broadcasted_iota(jnp.int32, (256, 1), 0)
    lane = m & 127
    spot = jnp.where(lane < 64, lane + 32, lane - 64) + jnp.where(m < 128, 96, jnp.where(lane < 64, 0, 192))
    void = (lane >= 125) | (lane < jnp.where(m < 128, 29, 3))
    index = jnp.where(void, -100000, spot).astype(f32)
    slope = (2.0 * (hat(place(column + 1), index) - hat(place(column - 1), index))).astype(bf16)
    value = (2.0 * hat(place(column), index)).astype(bf16)
    sides = row_winds(row_table[...], (left, HALO_ROWS, 16, LEFT_NUMBER), (right, HALO_ROWS, 32, RIGHT_NUMBER))
    wx = jnp.concatenate([winds[:, 0:128], sides[:, 0:128]], 1)
    wy = jnp.concatenate([winds[:, 128:256], sides[:, 128:256]], 1)
    gx[...] = (
        jnp.dot(split[:, 0:512], spread[...], preferred_element_type=f32)
        + jnp.dot(split[:, 512:1024], spread[...], preferred_element_type=f32)
        + jnp.dot(wx, slope, preferred_element_type=f32)
    )
    gy[...] = jnp.dot(wy, value, preferred_element_type=f32)

    def cut(ref, r):
        return jnp.stack([ref[8 * r : 8 * r + 8, 128 * p : 128 * p + 128] for p in range(PHASES)])

    first = cut(gy, 0)
    above, here = above_first(cut(gy, ROWS - 1)), first
    for r in range(ROWS):
        below = cut(gy, r + 1) if r < ROWS - 1 else below_last(first)
        b0[r] = cut(force0, r) + cut(gx, r) + (below - above)
        above, here = here, below
    b0[ROWS] = below_last(b0[0])

    for cycle in range(CYCLES):
        vcycle(0, x, b, cycle == 0)

    powers = own_number(own, OWN_ROWS, *OWN_NUMBER) + own_number(left, HALO_ROWS, *LEFT_NUMBER) + own_number(right, HALO_ROWS, *RIGHT_NUMBER)
    power = jnp.max(functools.reduce(jnp.maximum, powers), axis=0, keepdims=True) + (GAIN_EXP - IN_EXP)
    bound[...] = jnp.broadcast_to(jnp.exp2(power), (512, 384))
    scale = jnp.exp2(-power)
    lane = lax.broadcasted_iota(jnp.int32, (8, 128), 1)
    inside = (lane >= LEAD) & (lane < LEAD + 48)
    for s in range(ROWS // 2):
        for p in range(PHASES // 2):
            pair = [jnp.where(inside, x0[r, p], pltpu.roll(x0[r, p + 4], 64, 1)) for r in (2 * s, 2 * s + 1)]
            pair = jnp.concatenate(pair, 0) * scale
            high = pair.astype(bf16)
            split[16 * s : 16 * s + 16, 128 * p : 128 * p + 128] = high
            split[16 * s : 16 * s + 16, 512 + 128 * p : 640 + 128 * p] = (pair - high.astype(f32)).astype(bf16)
    block = jnp.dot(split[:, 0:512], collect[...], preferred_element_type=f32) + jnp.dot(
        split[:, 512:1024], collect[...], preferred_element_type=f32
    )
    for j in range(3):
        for r in range(ROWS):
            flat[pl.ds(512 * j + r, 8, stride=64), :] = block[8 * r : 8 * r + 8, 128 * j : 128 * j + 128]
    for j in range(3):
        out[:, 128 * j : 128 * j + 128] = flat[512 * j : 512 * j + 512, :]


PARAMS = dict(compiler_params=pltpu.CompilerParams(vmem_limit_bytes=40 * 1024 * 1024))


def core_own(own, interpret=False):
    return pl.pallas_call(
        own_kernel,
        out_shape=(
            jax.ShapeDtypeStruct((512, 1024), f32),
            jax.ShapeDtypeStruct((512, 128), bf16),
            jax.ShapeDtypeStruct((512, 256), bf16),
        ),
        scratch_shapes=[pltpu.VMEM((512, 768), bf16)],
        interpret=interpret,
        **PARAMS,
    )(own, jnp.asarray(spread_table()[256:640]))


def core(own, left, right, parts, interpret=False):
    grids = []
    for level in range(GRIDS):
        rows, phases, _ = shape_of(level)
        grids.append(pltpu.VMEM((rows + 1, phases, 8, 128), f32))
    table = spread_table()
    return pl.pallas_call(
        kernel,
        out_shape=(jax.ShapeDtypeStruct((512, 384), f32), jax.ShapeDtypeStruct((512, 384), f32)),
        scratch_shapes=grids
        + grids
        + [
            pltpu.VMEM((512, 1024), f32),
            pltpu.VMEM((512, 1024), f32),
            pltpu.VMEM((512, 1024), bf16),
            pltpu.VMEM((1536, 128), f32),
        ],
        interpret=interpret,
        **PARAMS,
    )(own, left, right, jnp.asarray(np.concatenate([table[0:256], table[640:896]])), jnp.asarray(collect_table()), *parts)


def parcel_kernel(lat_first, lon_first, increments_hbm, winds_hbm, out, odd, increments, ens_winds, sems):
    copies = [
        pltpu.make_async_copy(increments_hbm, increments, sems.at[0]),
        pltpu.make_async_copy(winds_hbm, ens_winds, sems.at[1]),
    ]
    for copy in copies:
        copy.start()
    for copy in copies:
        copy.wait()
    top = jnp.max(jnp.max(jnp.abs(increments[...]), axis=(0, 1)), axis=(0, 1), keepdims=True)
    gust = jnp.max(jnp.max(jnp.abs(ens_winds[...].astype(f32)), axis=(0, 1)), axis=(0, 1), keepdims=True)
    top = jnp.maximum(jnp.maximum(top, 8.0 * gust), 1e-30)
    power = jnp.ceil(jnp.log2(top))
    scale = jnp.exp2(IN_EXP - power)
    lat, lon = lat_first[0].astype(f32), lon_first[0].astype(f32)
    odd[...] = jnp.full(odd.shape, ((lon_first[0] + 48) // 96 % 2).astype(f32))
    lane = lax.broadcasted_iota(jnp.int32, (16, 128), 1)
    slot = lane // 32
    even = slot % 2 == 0
    for field in range(2):
        for k in range(8):
            d = 8 * field + k
            block = increments[field, k] * scale
            low, high = block[0:16], block[16:32]
            for at, c in ((0, 0), (80, 256)):
                out[d, at : at + 16, :] = jnp.where(even, low[:, c : c + 128], high[:, c : c + 128])
                out[d, at + 16 : at + 32, :] = jnp.where(even, high[:, c : c + 128], low[:, c : c + 128])
            low, high = low[:, 128:256], high[:, 128:256]
            on, back = pltpu.roll(high, 32, 1), pltpu.roll(high, 96, 1)
            u, v = ens_winds[0, k].astype(f32) * scale, ens_winds[1, k].astype(f32) * scale
            across, along = (v, -u) if field == 0 else (u, v)
            winds = jnp.concatenate([across, along], 0)
            winds = jnp.concatenate([winds, jnp.zeros((16, 32), f32)], 1)
            first = jnp.where(slot == 0, low, jnp.where(slot == 1, on, pltpu.roll(winds, 64, 1)))
            first = jnp.where(lane == 125, lat, jnp.where(lane == 126, lon, jnp.where(lane == 127, power, first)))
            last = jnp.where(slot == 3, low, jnp.where(slot == 2, back, pltpu.roll(winds, 96, 1)))
            last = jnp.where(lane == 0, lat, jnp.where(lane == 1, lon, jnp.where(lane == 2, power, last)))
            out[d, 32:48, :] = first
            out[d, 48:64, :] = jnp.where(slot == 0, back, jnp.where(slot == 3, on, low))
            out[d, 64:80, :] = last


def in_hbm(value):
    return pltpu.with_memory_space_constraint(value, pltpu.HBM)


def parcel(increments, ens_winds, lat_offsets, lon_offsets, interpret=False):
    scalar = pl.BlockSpec(memory_space=pltpu.SMEM)
    whole = pl.BlockSpec(memory_space=pltpu.HBM)
    return pl.pallas_call(
        parcel_kernel,
        out_shape=(
            jax.ShapeDtypeStruct((16, OWN_ROWS, 128), f32),
            jax.ShapeDtypeStruct((16, HALO_ROWS, 128), f32),
        ),
        in_specs=[scalar, scalar, whole, whole],
        scratch_shapes=[
            pltpu.VMEM(increments.shape, f32),
            pltpu.VMEM(ens_winds.shape, bf16),
            pltpu.SemaphoreType.DMA((2,)),
        ],
        interpret=interpret,
        **PARAMS,
    )(lat_offsets, lon_offsets, in_hbm(increments), in_hbm(ens_winds))


def local(increments, ens_winds, lat_offsets, lon_offsets):
    count = lax.axis_size("lon")
    mine, odd = parcel(increments, ens_winds, lat_offsets, lon_offsets)
    held = lax.all_to_all(mine.astype(jnp.float16), "lat", 0, 0, tiled=True)
    even = odd < 0.5
    to_left, to_right = held[:, 0:HALO_ROWS], held[:, OWN_ROWS - HALO_ROWS :]
    pairs0 = [(i, i ^ 1) for i in range(count)]
    pairs1 = [(i, (((i - 1) ^ 1) + 1) % count) for i in range(count)]
    got0 = lax.ppermute(jnp.where(even, to_right, to_left), "lon", pairs0)
    got1 = lax.ppermute(jnp.where(even, to_left, to_right), "lon", pairs1)
    own = held.astype(f32).reshape(16 * OWN_ROWS, 128)
    parts = core_own(own)
    got0 = lax.optimization_barrier(got0.astype(f32))
    got1 = got1.astype(f32)
    left = jnp.where(even, got1, got0).reshape(16 * HALO_ROWS, 128)
    right = jnp.where(even, got0, got1).reshape(16 * HALO_ROWS, 128)
    done, bound = core(own, left, right, parts)
    back = lax.all_to_all(done.astype(jnp.float16).reshape(16, 32, 384), "lat", 0, 0, tiled=True)
    return (back.astype(f32) * bound.reshape(back.shape)).reshape(increments.shape)


def solution(mesh):
    in_specs = (P(None, None, "lat", "lon"), P(None, None, "lat", "lon"), P("lat"), P("lon"))
    out_specs = P(None, None, "lat", "lon")
    return jax.shard_map(local, mesh=mesh, in_specs=in_specs, out_specs=out_specs, check_vma=False)
```

```python
import functools

import jax
import jax.numpy as jnp
import ml_dtypes
import numpy as np
from jax import lax
from jax.experimental import pallas as pl
from jax.experimental.pallas import tpu as pltpu
from jax.sharding import PartitionSpec as P

CLAT = 32
GRIDS = 5
OMEGA = 0.8
COARSE_SWEEPS = 4
CYCLES = 2
ROWS = 64
PHASES = 8
LEAD = 40
IN_EXP = 14.0
GAIN_EXP = 13.0
OWN_ROWS = 112
HALO_ROWS = 64

f32 = jnp.float32
bf16 = jnp.bfloat16


def column_of(n):
    return 8 * (n % 128 - LEAD) + n // 128


def spread_table():
    columns = column_of(np.arange(1024))
    return (np.arange(896)[:, None] - 256 == columns[None, :]).astype(ml_dtypes.bfloat16)


def collect_table():
    n = np.arange(512)
    phase, lane = n // 128, n % 128
    second = (lane < 24) | (lane >= 104)
    columns = np.where(second, 8 * ((lane + 64) % 128 - LEAD) + phase + 4, 8 * (lane - LEAD) + phase)
    columns = np.where(second | ((lane >= LEAD) & (lane < LEAD + 48)), columns, -1)
    return (columns[:, None] == np.arange(384)[None, :]).astype(ml_dtypes.bfloat16)


def centre(level):
    return 4.0 + 4.0**level * 0.25 / (CLAT * CLAT)


def west(v, hop):
    first = pltpu.roll(v[-1], hop, 1)[None]
    return jnp.concatenate([first, v[:-1]], 0) if v.shape[0] > 1 else first


def east(v, hop):
    last = pltpu.roll(v[0], 128 - hop, 1)[None]
    return jnp.concatenate([v[1:], last], 0) if v.shape[0] > 1 else last


def packed_west(v):
    middle = middle_lanes()
    first = jnp.where(middle, pltpu.roll(v[-1], 65, 1), pltpu.roll(v[-1], 64, 1))
    return jnp.concatenate([first[None], v[:-1]], 0)


def packed_east(v):
    middle = middle_lanes()
    last = jnp.where(middle, pltpu.roll(v[0], 64, 1), pltpu.roll(v[0], 63, 1))
    return jnp.concatenate([v[1:], last[None]], 0)


def middle_lanes():
    lane = lax.broadcasted_iota(jnp.int32, (8, 128), 1)
    return (lane >= 32) & (lane < 96)


def packed(v):
    half = PHASES // 2
    return jnp.concatenate([jnp.where(middle_lanes(), v[p], pltpu.roll(v[p + half], 64, 1))[None] for p in range(half)], 0)


def last_sweeps(x, b, coarse, y):
    gain = OMEGA / centre(0)
    old = lambda r: packed(x[r] + doubled(coarse[r // 2], PHASES))

    def run(old, b_of, last):
        first = old(0)
        prev, here = above_first(old(ROWS - 1)), first
        for r in range(ROWS):
            below = old(r + 1) if r < ROWS - 1 else below_last(first)
            near = (prev + below) + (packed_west(here) + packed_east(here))
            last(r, 0.2 * here + gain * (b_of(r) + near))
            prev, here = here, below

    def keep(r, value):
        y[r] = value

    def keep_b(r):
        y[ROWS + r] = packed(b[r])
        return y[ROWS + r]

    run(old, keep_b, keep)
    run(lambda r: y[r], lambda r: y[ROWS + r], keep)


def above_first(v):
    lanes = lax.broadcasted_iota(jnp.int32, (8, 128), 0)
    return jnp.stack([jnp.where(lanes > 0, pltpu.roll(v[p], 1, 0), 0.0) for p in range(v.shape[0])])


def below_last(v):
    lanes = lax.broadcasted_iota(jnp.int32, (8, 128), 0)
    return jnp.stack([jnp.where(lanes < 7, pltpu.roll(v[p], 7, 0), 0.0) for p in range(v.shape[0])])


def doubled(v, phases):
    if v.shape[0] == phases:
        return v
    return jnp.concatenate([v[p // 2][None] for p in range(phases)], 0)


def loop(count, body, carry, unroll):
    if unroll >= count:
        for step in range(count):
            carry = body(step, carry)
        return carry
    return lax.fori_loop(0, count, body, carry, unroll=unroll)


def shape_of(level):
    return ROWS >> level, max(PHASES >> level, 1), (2 if level == GRIDS - 1 else 1)


UNROLL = (32, 16, 8, 4, 2)


def sweep(level, x, b, start=False, coarse=None):
    rows, phases, hop = shape_of(level)
    gain = OMEGA / centre(level)
    if start:
        old = lambda r, s: b[r]
    elif coarse is not None:
        old = lambda r, s: x[r] + doubled(coarse[s], phases)
    else:
        old = lambda r, s: x[r]
    first = old(0, 0)
    top = above_first(old(rows - 1, rows // 2 - 1))
    if not start:
        x[rows] = below_last(first)

    def step(r, above, here, below):
        near = (above + below) + (west(here, hop) + east(here, hop))
        if start:
            return (1.2 * gain) * here + (gain * gain) * near
        return 0.2 * here + gain * (b[r] + near)

    def body(s, carry):
        prev, c0 = carry
        c1 = old(2 * s + 1, s)
        n = old(2 * s + 2, s + 1)
        x[2 * s] = step(2 * s, prev, c0, c1)
        x[2 * s + 1] = step(2 * s + 1, c0, c1, n)
        return c1, n

    loop(rows // 2, body, (top, first), UNROLL[level])


def residual(level, x, b, out):
    rows, phases, hop = shape_of(level)
    weight = 2.0 - centre(level)
    first = x[0]
    top = above_first(x[rows - 1])
    x[rows] = below_last(first)
    lane = lax.broadcasted_iota(jnp.int32, (8, 128), 1)

    def across(v):
        if phases > 1:
            return jnp.concatenate([(v[2 * p] + v[2 * p + 1])[None] for p in range(phases // 2)], 0)
        return v + jnp.where(lane % 2 == 0, pltpu.roll(v[0], 127, 1), pltpu.roll(v[0], 1, 1))[None]

    def sides(v):
        if phases > 1:
            to_west = jnp.concatenate([pltpu.roll(v[-1], 1, 1)[None]] + [v[2 * p - 1][None] for p in range(1, phases // 2)], 0)
            to_east = jnp.concatenate([v[2 * p][None] for p in range(1, phases // 2)] + [pltpu.roll(v[0], 127, 1)[None]], 0)
            return to_west + to_east
        near = jnp.where(lane % 2 == 0, pltpu.roll(v[0], 1, 1), pltpu.roll(v[0], 127, 1))
        far = jnp.where(lane % 2 == 0, pltpu.roll(v[0], 126, 1), pltpu.roll(v[0], 2, 1))
        return (near + far)[None]

    def body(s, carry):
        prev, c0 = carry
        c1 = x[2 * s + 1]
        n = x[2 * s + 2]
        flat_n = across(n)
        pair = c0 + c1
        out[s] = across(b[2 * s] + b[2 * s + 1]) + weight * across(pair) + ((prev + flat_n) + sides(pair))
        return across(c1), n

    loop(rows // 2, body, (across(top), first), UNROLL[level])
    out[rows // 2] = below_last(out[0])


def coarsest(x, b):
    level = GRIDS - 1
    rows, _, hop = shape_of(level)
    gain = OMEGA / centre(level)
    source = [b[r][0] for r in range(rows)]
    sub = lax.broadcasted_iota(jnp.int32, (8, 128), 0)
    v = source
    for turn in range(COARSE_SWEEPS - 1):
        above = [jnp.where(sub > 0, pltpu.roll(v[-1], 1, 0), 0.0)] + v[:-1]
        below = v[1:] + [jnp.where(sub < 7, pltpu.roll(v[0], 7, 0), 0.0)]
        near = [(above[r] + below[r]) + (pltpu.roll(v[r], hop, 1) + pltpu.roll(v[r], 128 - hop, 1)) for r in range(rows)]
        if turn == 0:
            v = [(1.2 * gain) * v[r] + (gain * gain) * near[r] for r in range(rows)]
        else:
            v = [0.2 * v[r] + gain * (source[r] + near[r]) for r in range(rows)]
    for r in range(rows):
        x[r] = v[r][None]
    x[rows] = jnp.zeros(x.shape[1:], f32)


def vcycle(level, x, b, fresh, last=None):
    if level == GRIDS - 1:
        coarsest(x[level], b[level])
        return
    if fresh:
        sweep(level, x[level], b[level], start=True)
    else:
        sweep(level, x[level], b[level])
        sweep(level, x[level], b[level])
    residual(level, x[level], b[level], b[level + 1])
    vcycle(level + 1, x, b, True)
    if last is not None:
        last_sweeps(x[level], b[level], x[level + 1], last)
        return
    sweep(level, x[level], b[level], coarse=x[level + 1])
    sweep(level, x[level], b[level])
    if level > 0:
        x[level][shape_of(level)[0]] = jnp.zeros(x[level].shape[1:], f32)


def hat(position, index):
    return jnp.maximum(1.0 - jnp.abs(position - index), 0.0)


def own_number(ref, height, at, lane):
    return [ref[pl.ds(height * half + at, 8, stride=2 * height), :][:, lane : lane + 1] for half in range(2)]


def spread_rows(split, sources, width):
    slot = lax.broadcasted_iota(jnp.int32, (8, 128), 1) // 32

    def put(j, s, pair):
        block = jnp.concatenate(pair, 0)
        high = block.astype(bf16)
        split[16 * s : 16 * s + 16, 128 * j : 128 * j + 128] = high
        split[16 * s : 16 * s + 16, width + 128 * j : width + 128 * j + 128] = (block - high.astype(f32)).astype(bf16)

    for j, (ref, height, units, number, outer) in enumerate(sources):
        scale = [jnp.exp2(k - IN_EXP) for k in own_number(ref, height, *number)]
        for half in range(2):
            rows = {}
            for a in range(16):
                get = lambda at: ref[pl.ds(height * half + at + a, 8, stride=2 * height), :] * scale[half]
                if outer:
                    one, two = get(units[0]), get(units[1])
                    rows[a] = jnp.where(slot % 2 == 0, one, two)
                    rows[a + 16] = jnp.where(slot % 2 == 0, two, one)
                else:
                    middle = get(units[1])
                    low = jnp.where((slot == 1) | (slot == 2), middle, 0.0)
                    high = jnp.where(slot == 1, pltpu.roll(middle, 32, 1), jnp.where(slot == 2, pltpu.roll(middle, 96, 1), 0.0))
                    if units[0] is not None:
                        one = get(units[0])
                        low = jnp.where(slot == 0, one, low)
                        high = jnp.where(slot == 0, pltpu.roll(one, 96, 1), high)
                    if units[2] is not None:
                        two = get(units[2])
                        low = jnp.where(slot == 3, two, low)
                        high = jnp.where(slot == 3, pltpu.roll(two, 32, 1), high)
                    rows[a] = low
                    rows[a + 16] = high
            for s in range(16):
                put(j, 16 * half + s, (rows[2 * s], rows[2 * s + 1]))


OWN_NUMBER = (32, 127)
RIGHT_NUMBER = (32, 127)
LEFT_NUMBER = (16, 2)


def row_winds(row_table, low, high):
    lane = lax.broadcasted_iota(jnp.int32, (8, 128), 1)
    both = []
    for offset in (0, 8):
        rows = []
        for i in range(16):
            parts = []
            for ref, height, at, number in (low, high):
                first = i * height + at
                number_row = i * height + number[0]
                scale = jnp.exp2(ref[number_row : number_row + 1, number[1] : number[1] + 1] - IN_EXP)
                parts.append(ref[first + offset : first + offset + 8, :] * scale)
            rows.append(jnp.where(lane < 64, parts[0], parts[1]))
        both.append(jnp.concatenate(rows, 0))
    table = jnp.concatenate(both, 1).astype(bf16)
    return jnp.dot(row_table, table, preferred_element_type=f32).astype(bf16)


def own_kernel(own, spread, force0, row_table, winds, split):
    spread_rows(
        split,
        (
            (own, OWN_ROWS, (0, 16), OWN_NUMBER, True),
            (own, OWN_ROWS, (32, 48, 64), OWN_NUMBER, False),
            (own, OWN_ROWS, (80, 96), OWN_NUMBER, True),
        ),
        384,
    )
    force0[...] = jnp.dot(split[:, 0:384], spread[...], preferred_element_type=f32) + jnp.dot(
        split[:, 384:768], spread[...], preferred_element_type=f32
    )
    lane = lax.broadcasted_iota(jnp.int32, (8, 128), 1).astype(f32)
    parts = []
    for first in own_number(own, OWN_ROWS, OWN_NUMBER[0], 125):
        for a in range(32):
            parts.append(hat(first + a * 0.25, lane))
    table = jnp.concatenate(parts, 0).astype(bf16)
    row_table[...] = table
    winds[...] = row_winds(table, (own, OWN_ROWS, 64, OWN_NUMBER), (own, OWN_ROWS, 32, OWN_NUMBER))


def kernel(own, left, right, spread, collect, force0, row_table, winds, out, bound, x0, x1, x2, x3, x4, b0, b1, b2, b3, b4, gx, gy, split, flat, y):
    x = (x0, x1, x2, x3, x4)
    b = (b0, b1, b2, b3, b4)
    spread_rows(
        split,
        (
            (left, HALO_ROWS, (None, 0, 16), LEFT_NUMBER, False),
            (left, HALO_ROWS, (32, 48), LEFT_NUMBER, True),
            (right, HALO_ROWS, (0, 16), RIGHT_NUMBER, True),
            (right, HALO_ROWS, (32, 48, None), RIGHT_NUMBER, False),
        ),
        512,
    )
    n = lax.broadcasted_iota(jnp.int32, (1, 1024), 1)
    column = 8 * ((n & 127) - LEAD) + (n >> 7)

    def shift_of(ref, at, lane):
        first = ref[at : at + 1, lane : lane + 1]
        return first - 96.0 * jnp.floor((first + 48.0) * (1.0 / 96.0))

    shifts = (shift_of(left, 16, 1), shift_of(own, 32, 126), shift_of(right, 32, 126))

    def place(c):
        return c.astype(f32) * 0.25 + 96.0 + jnp.where(c < 0, shifts[0], jnp.where(c < 384, shifts[1], shifts[2]))

    m = lax.broadcasted_iota(jnp.int32, (256, 1), 0)
    lane = m & 127
    spot = jnp.where(lane < 64, lane + 32, lane - 64) + jnp.where(m < 128, 96, jnp.where(lane < 64, 0, 192))
    void = (lane >= 125) | (lane < jnp.where(m < 128, 29, 3))
    index = jnp.where(void, -100000, spot).astype(f32)
    slope = (2.0 * (hat(place(column + 1), index) - hat(place(column - 1), index))).astype(bf16)
    value = (2.0 * hat(place(column), index)).astype(bf16)
    sides = row_winds(row_table[...], (left, HALO_ROWS, 16, LEFT_NUMBER), (right, HALO_ROWS, 32, RIGHT_NUMBER))
    wx = jnp.concatenate([winds[:, 0:128], sides[:, 0:128]], 1)
    wy = jnp.concatenate([winds[:, 128:256], sides[:, 128:256]], 1)
    gx[...] = (
        jnp.dot(split[:, 0:512], spread[...], preferred_element_type=f32)
        + jnp.dot(split[:, 512:1024], spread[...], preferred_element_type=f32)
        + jnp.dot(wx, slope, preferred_element_type=f32)
    )
    gy[...] = jnp.dot(wy, value, preferred_element_type=f32)

    def cut(ref, r):
        return jnp.stack([ref[8 * r : 8 * r + 8, 128 * p : 128 * p + 128] for p in range(PHASES)])

    first = cut(gy, 0)
    above, here = above_first(cut(gy, ROWS - 1)), first
    for r in range(ROWS):
        below = cut(gy, r + 1) if r < ROWS - 1 else below_last(first)
        b0[r] = cut(force0, r) + cut(gx, r) + (below - above)
        above, here = here, below
    b0[ROWS] = below_last(b0[0])

    for cycle in range(CYCLES):
        vcycle(0, x, b, cycle == 0, y if cycle == CYCLES - 1 else None)

    powers = own_number(own, OWN_ROWS, *OWN_NUMBER) + own_number(left, HALO_ROWS, *LEFT_NUMBER) + own_number(right, HALO_ROWS, *RIGHT_NUMBER)
    power = jnp.max(functools.reduce(jnp.maximum, powers), axis=0, keepdims=True) + (GAIN_EXP - IN_EXP)
    bound[...] = jnp.broadcast_to(jnp.exp2(power), (512, 384))
    scale = jnp.exp2(-power)
    for s in range(ROWS // 2):
        for p in range(PHASES // 2):
            pair = jnp.concatenate([y[2 * s, p], y[2 * s + 1, p]], 0) * scale
            high = pair.astype(bf16)
            split[16 * s : 16 * s + 16, 128 * p : 128 * p + 128] = high
            split[16 * s : 16 * s + 16, 512 + 128 * p : 640 + 128 * p] = (pair - high.astype(f32)).astype(bf16)
    block = jnp.dot(split[:, 0:512], collect[...], preferred_element_type=f32) + jnp.dot(
        split[:, 512:1024], collect[...], preferred_element_type=f32
    )
    for j in range(3):
        for r in range(ROWS):
            flat[pl.ds(512 * j + r, 8, stride=64), :] = block[8 * r : 8 * r + 8, 128 * j : 128 * j + 128]
    for j in range(3):
        out[:, 128 * j : 128 * j + 128] = flat[512 * j : 512 * j + 512, :]


PARAMS = dict(compiler_params=pltpu.CompilerParams(vmem_limit_bytes=40 * 1024 * 1024))


def core_own(own, interpret=False):
    return pl.pallas_call(
        own_kernel,
        out_shape=(
            jax.ShapeDtypeStruct((512, 1024), f32),
            jax.ShapeDtypeStruct((512, 128), bf16),
            jax.ShapeDtypeStruct((512, 256), bf16),
        ),
        scratch_shapes=[pltpu.VMEM((512, 768), bf16)],
        interpret=interpret,
        **PARAMS,
    )(own, jnp.asarray(spread_table()[256:640]))


def core(own, left, right, parts, interpret=False):
    grids = []
    for level in range(GRIDS):
        rows, phases, _ = shape_of(level)
        grids.append(pltpu.VMEM((rows + 1, phases, 8, 128), f32))
    table = spread_table()
    return pl.pallas_call(
        kernel,
        out_shape=(jax.ShapeDtypeStruct((512, 384), f32), jax.ShapeDtypeStruct((512, 384), f32)),
        scratch_shapes=grids
        + grids
        + [
            pltpu.VMEM((512, 1024), f32),
            pltpu.VMEM((512, 1024), f32),
            pltpu.VMEM((512, 1024), bf16),
            pltpu.VMEM((1536, 128), f32),
            pltpu.VMEM((2 * ROWS, PHASES // 2, 8, 128), f32),
        ],
        interpret=interpret,
        **PARAMS,
    )(own, left, right, jnp.asarray(np.concatenate([table[0:256], table[640:896]])), jnp.asarray(collect_table()), *parts)


def parcel_kernel(lat_first, lon_first, increments_hbm, winds_hbm, out, odd, increments, ens_winds, sems):
    copies = [
        pltpu.make_async_copy(increments_hbm, increments, sems.at[0]),
        pltpu.make_async_copy(winds_hbm, ens_winds, sems.at[1]),
    ]
    for copy in copies:
        copy.start()
    for copy in copies:
        copy.wait()
    top = jnp.max(jnp.max(jnp.abs(increments[...]), axis=(0, 1)), axis=(0, 1), keepdims=True)
    gust = jnp.max(jnp.max(jnp.abs(ens_winds[...].astype(f32)), axis=(0, 1)), axis=(0, 1), keepdims=True)
    top = jnp.maximum(jnp.maximum(top, 8.0 * gust), 1e-30)
    power = jnp.ceil(jnp.log2(top))
    scale = jnp.exp2(IN_EXP - power)
    lat, lon = lat_first[0].astype(f32), lon_first[0].astype(f32)
    odd[...] = jnp.full(odd.shape, ((lon_first[0] + 48) // 96 % 2).astype(f32))
    lane = lax.broadcasted_iota(jnp.int32, (16, 128), 1)
    slot = lane // 32
    even = slot % 2 == 0
    for field in range(2):
        for k in range(8):
            d = 8 * field + k
            block = increments[field, k] * scale
            low, high = block[0:16], block[16:32]
            for at, c in ((0, 0), (80, 256)):
                out[d, at : at + 16, :] = jnp.where(even, low[:, c : c + 128], high[:, c : c + 128])
                out[d, at + 16 : at + 32, :] = jnp.where(even, high[:, c : c + 128], low[:, c : c + 128])
            low, high = low[:, 128:256], high[:, 128:256]
            on, back = pltpu.roll(high, 32, 1), pltpu.roll(high, 96, 1)
            u, v = ens_winds[0, k].astype(f32) * scale, ens_winds[1, k].astype(f32) * scale
            across, along = (v, -u) if field == 0 else (u, v)
            winds = jnp.concatenate([across, along], 0)
            winds = jnp.concatenate([winds, jnp.zeros((16, 32), f32)], 1)
            first = jnp.where(slot == 0, low, jnp.where(slot == 1, on, pltpu.roll(winds, 64, 1)))
            first = jnp.where(lane == 125, lat, jnp.where(lane == 126, lon, jnp.where(lane == 127, power, first)))
            last = jnp.where(slot == 3, low, jnp.where(slot == 2, back, pltpu.roll(winds, 96, 1)))
            last = jnp.where(lane == 0, lat, jnp.where(lane == 1, lon, jnp.where(lane == 2, power, last)))
            out[d, 32:48, :] = first
            out[d, 48:64, :] = jnp.where(slot == 0, back, jnp.where(slot == 3, on, low))
            out[d, 64:80, :] = last


def in_hbm(value):
    return pltpu.with_memory_space_constraint(value, pltpu.HBM)


def parcel(increments, ens_winds, lat_offsets, lon_offsets, interpret=False):
    scalar = pl.BlockSpec(memory_space=pltpu.SMEM)
    whole = pl.BlockSpec(memory_space=pltpu.HBM)
    return pl.pallas_call(
        parcel_kernel,
        out_shape=(
            jax.ShapeDtypeStruct((16, OWN_ROWS, 128), f32),
            jax.ShapeDtypeStruct((16, HALO_ROWS, 128), f32),
        ),
        in_specs=[scalar, scalar, whole, whole],
        scratch_shapes=[
            pltpu.VMEM(increments.shape, f32),
            pltpu.VMEM(ens_winds.shape, bf16),
            pltpu.SemaphoreType.DMA((2,)),
        ],
        interpret=interpret,
        **PARAMS,
    )(lat_offsets, lon_offsets, in_hbm(increments), in_hbm(ens_winds))


def local(increments, ens_winds, lat_offsets, lon_offsets):
    count = lax.axis_size("lon")
    mine, odd = parcel(increments, ens_winds, lat_offsets, lon_offsets)
    held = lax.all_to_all(mine.astype(jnp.float16), "lat", 0, 0, tiled=True)
    even = odd < 0.5
    to_left, to_right = held[:, 0:HALO_ROWS], held[:, OWN_ROWS - HALO_ROWS :]
    pairs0 = [(i, i ^ 1) for i in range(count)]
    pairs1 = [(i, (((i - 1) ^ 1) + 1) % count) for i in range(count)]
    got0 = lax.ppermute(jnp.where(even, to_right, to_left), "lon", pairs0)
    got1 = lax.ppermute(jnp.where(even, to_left, to_right), "lon", pairs1)
    own = held.astype(f32).reshape(16 * OWN_ROWS, 128)
    parts = core_own(own)
    got0 = lax.optimization_barrier(got0.astype(f32))
    got1 = got1.astype(f32)
    left = jnp.where(even, got1, got0).reshape(16 * HALO_ROWS, 128)
    right = jnp.where(even, got0, got1).reshape(16 * HALO_ROWS, 128)
    done, bound = core(own, left, right, parts)
    back = lax.all_to_all(done.astype(jnp.float16).reshape(16, 32, 384), "lat", 0, 0, tiled=True)
    return (back.astype(f32) * bound.reshape(back.shape)).reshape(increments.shape)


def solution(mesh):
    in_specs = (P(None, None, "lat", "lon"), P(None, None, "lat", "lon"), P("lat"), P("lon"))
    out_specs = P(None, None, "lat", "lon")
    return jax.shard_map(local, mesh=mesh, in_specs=in_specs, out_specs=out_specs, check_vma=False)
```

```python
import functools

import jax
import jax.numpy as jnp
import ml_dtypes
import numpy as np
from jax import lax
from jax.experimental import pallas as pl
from jax.experimental.pallas import tpu as pltpu
from jax.sharding import PartitionSpec as P

CLAT = 32
GRIDS = 5
OMEGA = 0.8
COARSE_SWEEPS = 4
CYCLES = 2
ROWS = 64
PHASES = 8
LEAD = 40
IN_EXP = 14.0
GAIN_EXP = 13.0
OWN_ROWS = 112
HALO_ROWS = 64

f32 = jnp.float32
bf16 = jnp.bfloat16


def column_of(n):
    return 8 * (n % 128 - LEAD) + n // 128


def spread_table():
    columns = column_of(np.arange(1024))
    return (np.arange(896)[:, None] - 256 == columns[None, :]).astype(ml_dtypes.bfloat16)


def collect_table():
    n = np.arange(512)
    phase, lane = n // 128, n % 128
    second = (lane < 24) | (lane >= 104)
    columns = np.where(second, 8 * ((lane + 64) % 128 - LEAD) + phase + 4, 8 * (lane - LEAD) + phase)
    columns = np.where(second | ((lane >= LEAD) & (lane < LEAD + 48)), columns, -1)
    return (columns[:, None] == np.arange(384)[None, :]).astype(ml_dtypes.bfloat16)


def centre(level):
    return 4.0 + 4.0**level * 0.25 / (CLAT * CLAT)


def west(v, hop):
    first = pltpu.roll(v[-1], hop, 1)[None]
    return jnp.concatenate([first, v[:-1]], 0) if v.shape[0] > 1 else first


def east(v, hop):
    last = pltpu.roll(v[0], 128 - hop, 1)[None]
    return jnp.concatenate([v[1:], last], 0) if v.shape[0] > 1 else last


def packed_west(v):
    middle = middle_lanes()
    first = jnp.where(middle, pltpu.roll(v[-1], 65, 1), pltpu.roll(v[-1], 64, 1))
    return jnp.concatenate([first[None], v[:-1]], 0)


def packed_east(v):
    middle = middle_lanes()
    last = jnp.where(middle, pltpu.roll(v[0], 64, 1), pltpu.roll(v[0], 63, 1))
    return jnp.concatenate([v[1:], last[None]], 0)


def middle_lanes():
    lane = lax.broadcasted_iota(jnp.int32, (8, 128), 1)
    return (lane >= 32) & (lane < 96)


def packed(v):
    half = v.shape[0] // 2
    return jnp.concatenate([jnp.where(middle_lanes(), v[p], pltpu.roll(v[p + half], 64, 1))[None] for p in range(half)], 0)


def last_sweeps(level, x, b, coarse, y):
    rows, phases, _ = shape_of(level)
    gain = OMEGA / centre(level)
    if level == 0:
        old = lambda r: packed(x[r]) + doubled(coarse[r // 2], phases // 2)
    else:
        old = lambda r: packed(x[r] + doubled(coarse[r // 2], phases))

    def run(old, b_of, last):
        first = old(0)
        prev, here = above_first(old(rows - 1)), first
        for r in range(rows):
            below = old(r + 1) if r < rows - 1 else below_last(first)
            near = (prev + below) + (packed_west(here) + packed_east(here))
            last(r, 0.2 * here + gain * (b_of(r) + near))
            prev, here = here, below

    def keep(r, value):
        y[r] = value

    def keep_b(r):
        y[rows + r] = packed(b[r])
        return y[rows + r]

    run(old, keep_b, keep)
    run(lambda r: y[r], lambda r: y[rows + r], keep)


def above_first(v):
    lanes = lax.broadcasted_iota(jnp.int32, (8, 128), 0)
    return jnp.stack([jnp.where(lanes > 0, pltpu.roll(v[p], 1, 0), 0.0) for p in range(v.shape[0])])


def below_last(v):
    lanes = lax.broadcasted_iota(jnp.int32, (8, 128), 0)
    return jnp.stack([jnp.where(lanes < 7, pltpu.roll(v[p], 7, 0), 0.0) for p in range(v.shape[0])])


def doubled(v, phases):
    if v.shape[0] == phases:
        return v
    return jnp.concatenate([v[p // 2][None] for p in range(phases)], 0)


def loop(count, body, carry, unroll):
    if unroll >= count:
        for step in range(count):
            carry = body(step, carry)
        return carry
    return lax.fori_loop(0, count, body, carry, unroll=unroll)


def shape_of(level):
    return ROWS >> level, max(PHASES >> level, 1), (2 if level == GRIDS - 1 else 1)


UNROLL = (32, 16, 8, 4, 2)


def sweep(level, x, b, start=False, coarse=None):
    rows, phases, hop = shape_of(level)
    gain = OMEGA / centre(level)
    if start:
        old = lambda r, s: b[r]
    elif coarse is not None:
        old = lambda r, s: x[r] + doubled(coarse[s], phases)
    else:
        old = lambda r, s: x[r]
    first = old(0, 0)
    top = above_first(old(rows - 1, rows // 2 - 1))
    if not start:
        x[rows] = below_last(first)

    def step(r, above, here, below):
        near = (above + below) + (west(here, hop) + east(here, hop))
        if start:
            return (1.2 * gain) * here + (gain * gain) * near
        return 0.2 * here + gain * (b[r] + near)

    def body(s, carry):
        prev, c0 = carry
        c1 = old(2 * s + 1, s)
        n = old(2 * s + 2, s + 1)
        x[2 * s] = step(2 * s, prev, c0, c1)
        x[2 * s + 1] = step(2 * s + 1, c0, c1, n)
        return c1, n

    loop(rows // 2, body, (top, first), UNROLL[level])


def residual(level, x, b, out):
    rows, phases, hop = shape_of(level)
    weight = 2.0 - centre(level)
    first = x[0]
    top = above_first(x[rows - 1])
    x[rows] = below_last(first)
    lane = lax.broadcasted_iota(jnp.int32, (8, 128), 1)

    def across(v):
        if phases > 1:
            return jnp.concatenate([(v[2 * p] + v[2 * p + 1])[None] for p in range(phases // 2)], 0)
        return v + jnp.where(lane % 2 == 0, pltpu.roll(v[0], 127, 1), pltpu.roll(v[0], 1, 1))[None]

    def sides(v):
        if phases > 1:
            to_west = jnp.concatenate([pltpu.roll(v[-1], 1, 1)[None]] + [v[2 * p - 1][None] for p in range(1, phases // 2)], 0)
            to_east = jnp.concatenate([v[2 * p][None] for p in range(1, phases // 2)] + [pltpu.roll(v[0], 127, 1)[None]], 0)
            return to_west + to_east
        near = jnp.where(lane % 2 == 0, pltpu.roll(v[0], 1, 1), pltpu.roll(v[0], 127, 1))
        far = jnp.where(lane % 2 == 0, pltpu.roll(v[0], 126, 1), pltpu.roll(v[0], 2, 1))
        return (near + far)[None]

    def body(s, carry):
        prev, c0 = carry
        c1 = x[2 * s + 1]
        n = x[2 * s + 2]
        flat_n = across(n)
        pair = c0 + c1
        out[s] = across(b[2 * s] + b[2 * s + 1]) + weight * across(pair) + ((prev + flat_n) + sides(pair))
        return across(c1), n

    loop(rows // 2, body, (across(top), first), UNROLL[level])
    out[rows // 2] = below_last(out[0])


def coarsest(x, b):
    level = GRIDS - 1
    rows, _, hop = shape_of(level)
    gain = OMEGA / centre(level)
    source = [b[r][0] for r in range(rows)]
    sub = lax.broadcasted_iota(jnp.int32, (8, 128), 0)
    v = source
    for turn in range(COARSE_SWEEPS - 1):
        above = [jnp.where(sub > 0, pltpu.roll(v[-1], 1, 0), 0.0)] + v[:-1]
        below = v[1:] + [jnp.where(sub < 7, pltpu.roll(v[0], 7, 0), 0.0)]
        near = [(above[r] + below[r]) + (pltpu.roll(v[r], hop, 1) + pltpu.roll(v[r], 128 - hop, 1)) for r in range(rows)]
        if turn == 0:
            v = [(1.2 * gain) * v[r] + (gain * gain) * near[r] for r in range(rows)]
        else:
            v = [0.2 * v[r] + gain * (source[r] + near[r]) for r in range(rows)]
    for r in range(rows):
        x[r] = v[r][None]
    x[rows] = jnp.zeros(x.shape[1:], f32)


def vcycle(level, x, b, fresh, last=None):
    if level == GRIDS - 1:
        coarsest(x[level], b[level])
        return
    if fresh:
        sweep(level, x[level], b[level], start=True)
    else:
        sweep(level, x[level], b[level])
        sweep(level, x[level], b[level])
    residual(level, x[level], b[level], b[level + 1])
    vcycle(level + 1, x, b, True, last[1:] if last else None)
    if last:
        last_sweeps(level, x[level], b[level], last[1] if level == 0 else x[level + 1], last[0])
        return
    sweep(level, x[level], b[level], coarse=x[level + 1])
    sweep(level, x[level], b[level])
    if level > 0:
        x[level][shape_of(level)[0]] = jnp.zeros(x[level].shape[1:], f32)


def hat(position, index):
    return jnp.maximum(1.0 - jnp.abs(position - index), 0.0)


def own_number(ref, height, at, lane):
    return [ref[pl.ds(height * half + at, 8, stride=2 * height), :][:, lane : lane + 1] for half in range(2)]


def spread_rows(split, sources, width):
    slot = lax.broadcasted_iota(jnp.int32, (8, 128), 1) // 32

    def put(j, s, pair):
        block = jnp.concatenate(pair, 0)
        high = block.astype(bf16)
        split[16 * s : 16 * s + 16, 128 * j : 128 * j + 128] = high
        split[16 * s : 16 * s + 16, width + 128 * j : width + 128 * j + 128] = (block - high.astype(f32)).astype(bf16)

    for j, (ref, height, units, number, outer) in enumerate(sources):
        scale = [jnp.exp2(k - IN_EXP) for k in own_number(ref, height, *number)]
        for half in range(2):
            rows = {}
            for a in range(16):
                get = lambda at: ref[pl.ds(height * half + at + a, 8, stride=2 * height), :] * scale[half]
                if outer:
                    one, two = get(units[0]), get(units[1])
                    rows[a] = jnp.where(slot % 2 == 0, one, two)
                    rows[a + 16] = jnp.where(slot % 2 == 0, two, one)
                else:
                    middle = get(units[1])
                    low = jnp.where((slot == 1) | (slot == 2), middle, 0.0)
                    high = jnp.where(slot == 1, pltpu.roll(middle, 32, 1), jnp.where(slot == 2, pltpu.roll(middle, 96, 1), 0.0))
                    if units[0] is not None:
                        one = get(units[0])
                        low = jnp.where(slot == 0, one, low)
                        high = jnp.where(slot == 0, pltpu.roll(one, 96, 1), high)
                    if units[2] is not None:
                        two = get(units[2])
                        low = jnp.where(slot == 3, two, low)
                        high = jnp.where(slot == 3, pltpu.roll(two, 32, 1), high)
                    rows[a] = low
                    rows[a + 16] = high
            for s in range(16):
                put(j, 16 * half + s, (rows[2 * s], rows[2 * s + 1]))


OWN_NUMBER = (32, 127)
RIGHT_NUMBER = (32, 127)
LEFT_NUMBER = (16, 2)


def row_winds(row_table, low, high):
    lane = lax.broadcasted_iota(jnp.int32, (8, 128), 1)
    both = []
    for offset in (0, 8):
        rows = []
        for i in range(16):
            parts = []
            for ref, height, at, number in (low, high):
                first = i * height + at
                number_row = i * height + number[0]
                scale = jnp.exp2(ref[number_row : number_row + 1, number[1] : number[1] + 1] - IN_EXP)
                parts.append(ref[first + offset : first + offset + 8, :] * scale)
            rows.append(jnp.where(lane < 64, parts[0], parts[1]))
        both.append(jnp.concatenate(rows, 0))
    table = jnp.concatenate(both, 1).astype(bf16)
    return jnp.dot(row_table, table, preferred_element_type=f32).astype(bf16)


def own_kernel(own, spread, force0, row_table, winds, split):
    spread_rows(
        split,
        (
            (own, OWN_ROWS, (0, 16), OWN_NUMBER, True),
            (own, OWN_ROWS, (32, 48, 64), OWN_NUMBER, False),
            (own, OWN_ROWS, (80, 96), OWN_NUMBER, True),
        ),
        384,
    )
    force0[...] = jnp.dot(split[:, 0:384], spread[...], preferred_element_type=f32) + jnp.dot(
        split[:, 384:768], spread[...], preferred_element_type=f32
    )
    lane = lax.broadcasted_iota(jnp.int32, (8, 128), 1).astype(f32)
    parts = []
    for first in own_number(own, OWN_ROWS, OWN_NUMBER[0], 125):
        for a in range(32):
            parts.append(hat(first + a * 0.25, lane))
    table = jnp.concatenate(parts, 0).astype(bf16)
    row_table[...] = table
    winds[...] = row_winds(table, (own, OWN_ROWS, 64, OWN_NUMBER), (own, OWN_ROWS, 32, OWN_NUMBER))


def kernel(own, left, right, spread, collect, force0, row_table, winds, out, bound, x0, x1, x2, x3, x4, b0, b1, b2, b3, b4, gx, gy, split, flat, y, y1):
    x = (x0, x1, x2, x3, x4)
    b = (b0, b1, b2, b3, b4)
    spread_rows(
        split,
        (
            (left, HALO_ROWS, (None, 0, 16), LEFT_NUMBER, False),
            (left, HALO_ROWS, (32, 48), LEFT_NUMBER, True),
            (right, HALO_ROWS, (0, 16), RIGHT_NUMBER, True),
            (right, HALO_ROWS, (32, 48, None), RIGHT_NUMBER, False),
        ),
        512,
    )
    n = lax.broadcasted_iota(jnp.int32, (1, 1024), 1)
    column = 8 * ((n & 127) - LEAD) + (n >> 7)

    def shift_of(ref, at, lane):
        first = ref[at : at + 1, lane : lane + 1]
        return first - 96.0 * jnp.floor((first + 48.0) * (1.0 / 96.0))

    shifts = (shift_of(left, 16, 1), shift_of(own, 32, 126), shift_of(right, 32, 126))

    def place(c):
        return c.astype(f32) * 0.25 + 96.0 + jnp.where(c < 0, shifts[0], jnp.where(c < 384, shifts[1], shifts[2]))

    m = lax.broadcasted_iota(jnp.int32, (256, 1), 0)
    lane = m & 127
    spot = jnp.where(lane < 64, lane + 32, lane - 64) + jnp.where(m < 128, 96, jnp.where(lane < 64, 0, 192))
    void = (lane >= 125) | (lane < jnp.where(m < 128, 29, 3))
    index = jnp.where(void, -100000, spot).astype(f32)
    slope = (2.0 * (hat(place(column + 1), index) - hat(place(column - 1), index))).astype(bf16)
    value = (2.0 * hat(place(column), index)).astype(bf16)
    sides = row_winds(row_table[...], (left, HALO_ROWS, 16, LEFT_NUMBER), (right, HALO_ROWS, 32, RIGHT_NUMBER))
    wx = jnp.concatenate([winds[:, 0:128], sides[:, 0:128]], 1)
    wy = jnp.concatenate([winds[:, 128:256], sides[:, 128:256]], 1)
    gx[...] = (
        jnp.dot(split[:, 0:512], spread[...], preferred_element_type=f32)
        + jnp.dot(split[:, 512:1024], spread[...], preferred_element_type=f32)
        + jnp.dot(wx, slope, preferred_element_type=f32)
    )
    gy[...] = jnp.dot(wy, value, preferred_element_type=f32)

    def cut(ref, r):
        return jnp.stack([ref[8 * r : 8 * r + 8, 128 * p : 128 * p + 128] for p in range(PHASES)])

    first = cut(gy, 0)
    above, here = above_first(cut(gy, ROWS - 1)), first
    for r in range(ROWS):
        below = cut(gy, r + 1) if r < ROWS - 1 else below_last(first)
        b0[r] = cut(force0, r) + cut(gx, r) + (below - above)
        above, here = here, below
    b0[ROWS] = below_last(b0[0])

    for cycle in range(CYCLES):
        vcycle(0, x, b, cycle == 0, (y, y1) if cycle == CYCLES - 1 else None)

    powers = own_number(own, OWN_ROWS, *OWN_NUMBER) + own_number(left, HALO_ROWS, *LEFT_NUMBER) + own_number(right, HALO_ROWS, *RIGHT_NUMBER)
    power = jnp.max(functools.reduce(jnp.maximum, powers), axis=0, keepdims=True) + (GAIN_EXP - IN_EXP)
    bound[...] = jnp.broadcast_to(jnp.exp2(power), (512, 384))
    scale = jnp.exp2(-power)
    for s in range(ROWS // 2):
        for p in range(PHASES // 2):
            pair = jnp.concatenate([y[2 * s, p], y[2 * s + 1, p]], 0) * scale
            high = pair.astype(bf16)
            split[16 * s : 16 * s + 16, 128 * p : 128 * p + 128] = high
            split[16 * s : 16 * s + 16, 512 + 128 * p : 640 + 128 * p] = (pair - high.astype(f32)).astype(bf16)
    block = jnp.dot(split[:, 0:512], collect[...], preferred_element_type=f32) + jnp.dot(
        split[:, 512:1024], collect[...], preferred_element_type=f32
    )
    for j in range(3):
        for r in range(ROWS):
            flat[pl.ds(512 * j + r, 8, stride=64), :] = block[8 * r : 8 * r + 8, 128 * j : 128 * j + 128]
    for j in range(3):
        out[:, 128 * j : 128 * j + 128] = flat[512 * j : 512 * j + 512, :]


PARAMS = dict(compiler_params=pltpu.CompilerParams(vmem_limit_bytes=40 * 1024 * 1024))


def core_own(own, interpret=False):
    return pl.pallas_call(
        own_kernel,
        out_shape=(
            jax.ShapeDtypeStruct((512, 1024), f32),
            jax.ShapeDtypeStruct((512, 128), bf16),
            jax.ShapeDtypeStruct((512, 256), bf16),
        ),
        scratch_shapes=[pltpu.VMEM((512, 768), bf16)],
        interpret=interpret,
        **PARAMS,
    )(own, jnp.asarray(spread_table()[256:640]))


def core(own, left, right, parts, interpret=False):
    grids = []
    for level in range(GRIDS):
        rows, phases, _ = shape_of(level)
        grids.append(pltpu.VMEM((rows + 1, phases, 8, 128), f32))
    table = spread_table()
    return pl.pallas_call(
        kernel,
        out_shape=(jax.ShapeDtypeStruct((512, 384), f32), jax.ShapeDtypeStruct((512, 384), f32)),
        scratch_shapes=grids
        + grids
        + [
            pltpu.VMEM((512, 1024), f32),
            pltpu.VMEM((512, 1024), f32),
            pltpu.VMEM((512, 1024), bf16),
            pltpu.VMEM((1536, 128), f32),
            pltpu.VMEM((2 * ROWS, PHASES // 2, 8, 128), f32),
            pltpu.VMEM((ROWS, PHASES // 4, 8, 128), f32),
        ],
        interpret=interpret,
        **PARAMS,
    )(own, left, right, jnp.asarray(np.concatenate([table[0:256], table[640:896]])), jnp.asarray(collect_table()), *parts)


def parcel_kernel(lat_first, lon_first, increments_hbm, winds_hbm, out, odd, increments, ens_winds, sems):
    copies = [
        pltpu.make_async_copy(increments_hbm, increments, sems.at[0]),
        pltpu.make_async_copy(winds_hbm, ens_winds, sems.at[1]),
    ]
    for copy in copies:
        copy.start()
    for copy in copies:
        copy.wait()
    top = jnp.max(jnp.max(jnp.abs(increments[...]), axis=(0, 1)), axis=(0, 1), keepdims=True)
    gust = jnp.max(jnp.max(jnp.abs(ens_winds[...].astype(f32)), axis=(0, 1)), axis=(0, 1), keepdims=True)
    top = jnp.maximum(jnp.maximum(top, 8.0 * gust), 1e-30)
    power = jnp.ceil(jnp.log2(top))
    scale = jnp.exp2(IN_EXP - power)
    lat, lon = lat_first[0].astype(f32), lon_first[0].astype(f32)
    odd[...] = jnp.full(odd.shape, ((lon_first[0] + 48) // 96 % 2).astype(f32))
    lane = lax.broadcasted_iota(jnp.int32, (16, 128), 1)
    slot = lane // 32
    even = slot % 2 == 0
    for field in range(2):
        for k in range(8):
            d = 8 * field + k
            block = increments[field, k] * scale
            low, high = block[0:16], block[16:32]
            for at, c in ((0, 0), (80, 256)):
                out[d, at : at + 16, :] = jnp.where(even, low[:, c : c + 128], high[:, c : c + 128])
                out[d, at + 16 : at + 32, :] = jnp.where(even, high[:, c : c + 128], low[:, c : c + 128])
            low, high = low[:, 128:256], high[:, 128:256]
            on, back = pltpu.roll(high, 32, 1), pltpu.roll(high, 96, 1)
            u, v = ens_winds[0, k].astype(f32) * scale, ens_winds[1, k].astype(f32) * scale
            across, along = (v, -u) if field == 0 else (u, v)
            winds = jnp.concatenate([across, along], 0)
            winds = jnp.concatenate([winds, jnp.zeros((16, 32), f32)], 1)
            first = jnp.where(slot == 0, low, jnp.where(slot == 1, on, pltpu.roll(winds, 64, 1)))
            first = jnp.where(lane == 125, lat, jnp.where(lane == 126, lon, jnp.where(lane == 127, power, first)))
            last = jnp.where(slot == 3, low, jnp.where(slot == 2, back, pltpu.roll(winds, 96, 1)))
            last = jnp.where(lane == 0, lat, jnp.where(lane == 1, lon, jnp.where(lane == 2, power, last)))
            out[d, 32:48, :] = first
            out[d, 48:64, :] = jnp.where(slot == 0, back, jnp.where(slot == 3, on, low))
            out[d, 64:80, :] = last


def in_hbm(value):
    return pltpu.with_memory_space_constraint(value, pltpu.HBM)


def parcel(increments, ens_winds, lat_offsets, lon_offsets, interpret=False):
    scalar = pl.BlockSpec(memory_space=pltpu.SMEM)
    whole = pl.BlockSpec(memory_space=pltpu.HBM)
    return pl.pallas_call(
        parcel_kernel,
        out_shape=(
            jax.ShapeDtypeStruct((16, OWN_ROWS, 128), f32),
            jax.ShapeDtypeStruct((16, HALO_ROWS, 128), f32),
        ),
        in_specs=[scalar, scalar, whole, whole],
        scratch_shapes=[
            pltpu.VMEM(increments.shape, f32),
            pltpu.VMEM(ens_winds.shape, bf16),
            pltpu.SemaphoreType.DMA((2,)),
        ],
        interpret=interpret,
        **PARAMS,
    )(lat_offsets, lon_offsets, in_hbm(increments), in_hbm(ens_winds))


def local(increments, ens_winds, lat_offsets, lon_offsets):
    count = lax.axis_size("lon")
    mine, odd = parcel(increments, ens_winds, lat_offsets, lon_offsets)
    held = lax.all_to_all(mine.astype(jnp.float16), "lat", 0, 0, tiled=True)
    even = odd < 0.5
    to_left, to_right = held[:, 0:HALO_ROWS], held[:, OWN_ROWS - HALO_ROWS :]
    pairs0 = [(i, i ^ 1) for i in range(count)]
    pairs1 = [(i, (((i - 1) ^ 1) + 1) % count) for i in range(count)]
    got0 = lax.ppermute(jnp.where(even, to_right, to_left), "lon", pairs0)
    got1 = lax.ppermute(jnp.where(even, to_left, to_right), "lon", pairs1)
    own = held.astype(f32).reshape(16 * OWN_ROWS, 128)
    parts = core_own(own)
    got0 = lax.optimization_barrier(got0.astype(f32))
    got1 = got1.astype(f32)
    left = jnp.where(even, got1, got0).reshape(16 * HALO_ROWS, 128)
    right = jnp.where(even, got0, got1).reshape(16 * HALO_ROWS, 128)
    done, bound = core(own, left, right, parts)
    back = lax.all_to_all(done.astype(jnp.float16).reshape(16, 32, 384), "lat", 0, 0, tiled=True)
    return (back.astype(f32) * bound.reshape(back.shape)).reshape(increments.shape)


def solution(mesh):
    in_specs = (P(None, None, "lat", "lon"), P(None, None, "lat", "lon"), P("lat"), P("lon"))
    out_specs = P(None, None, "lat", "lon")
    return jax.shard_map(local, mesh=mesh, in_specs=in_specs, out_specs=out_specs, check_vma=False)
```
